128 devices in a mesh: gx: 16 (over z, x), gy: 8 (over y, core).
Axes of the slice: x: 4, y: 4, z: 4, core: 2. Of those that a mesh axis runs over, the one named last changes fastest.
Arguments:
- grid_now: float32 [3, 256, 256, 512], P(None, 'gx', 'gy'), may hold values from -6 to 6
- grid_before: float32 [3, 256, 256, 512], P(None, 'gx', 'gy'), may hold values from -6 to 6
- wave_factor: float32 [256, 256, 512], P('gx', 'gy'), may hold values from 0.04 to 0.2
- layer_owner: int32 [16, 4096, 1], P('gx', 'gy'), may hold values from 0 to 127; in each aligned block of 512 rows (0 to 511, 512 to 1023, ..., all dimensions but the last counted through in order) at most 8 rows name the same one
- layer_cell: int32 [16, 4096], P('gx', 'gy'), may hold values from 0 to 262143
- box_now: float32 [3, 16, 71680], P(None, 'gx', 'gy'), may hold values from -6 to 6
- box_before: float32 [3, 16, 71680], P(None, 'gx', 'gy'), may hold values from -6 to 6
- node_mass: float32 [16, 71680], P('gx', 'gy'), may hold values from 0.5 to 2
- corner_nodes: int32 [8, 16, 65536], P(None, 'gx', 'gy'), may hold values from 0 to 71679, as said below
- live_counts: int32 [16, 8], P('gx', 'gy'), may hold values from 2048 to 8192, as said below
- shear_modulus: float32 [16, 65536], P('gx', 'gy'), may hold values from 0.25 to 2
- lame_lambda: float32 [16, 65536], P('gx', 'gy'), may hold values from 0.5 to 4
- strain_scale: float32 [16, 65536], P('gx', 'gy'), may hold values from 0.2 to 2
- layer_nodes: int32 [16, 4096], P('gx', 'gy'), may hold values from 0 to 71679, as said below
Outputs:
- grid_after: float32 [3, 256, 256, 512], P(None, 'gx', 'gy')
- box_after: float32 [3, 16, 71680], P(None, 'gx', 'gy')
The draws below stay inside these ranges and needn't reach their ends.
Inputs may be any that keep to these rules, and one draw needn't show every extreme that they name: `layer_owner`: owners are numbered gx index times 8 plus gy index; among the 512 layer slots of one device at most 8 name the same owner. `layer_cell`: cells are numbered (x * 32 + y) * 512 + z within the owner's block. `corner_nodes`: corner a of an element sits at offsets (a % 2, a // 2 % 2, a // 4) of a unit cube; for each corner a, distinct element slots of a box name distinct nodes. `live_counts`: live slots come first in each device's block of 8192 slots. `layer_nodes`: the layer nodes of one box are distinct.
All inputs are finite; a program needn't handle non-finite values.
Results may differ from the reference program's by a relative error of at most 0.0003.
Values sent between devices are 32-bit elements; how exact they have to be, the bound alone decides.
A program may use at most 384 MiB of HBM per device.

```python
import math
import jax
import jax.numpy as jnp
import numpy as np
from jax import lax

CX = 16
CY = 32
NZ = 512
BY = 32
E_DEV = 8192
LAYER_DEV = 512
NX = 256
NY = 256
CELLS_DEV = 262144
BOXES = 16
BOX_ELEMS = 65536
BZ = 64
NODES = 70785
BOX_NODES = 71680
LAYER = 4096
CAP = 8
N_GY = 8
DEVICES = 128


def place_value(labels, target, spot):
    found = jnp.argmax(labels == target).astype(jnp.int32)
    held = labels[spot]
    return labels.at[found].set(held).at[spot].set(target)


def spread_labels(key, used):
    labels = jax.random.permutation(jax.random.fold_in(key, 1), BOX_NODES).astype(jnp.int32)
    first_spot = jax.random.randint(jax.random.fold_in(key, 3), (), 0, used).astype(jnp.int32)
    step_spot = jax.random.randint(jax.random.fold_in(key, 4), (), 1, used).astype(jnp.int32)
    second_spot = (first_spot + step_spot) % used
    labels = place_value(labels, BOX_NODES - 1, first_spot)
    labels = place_value(labels, 0, second_spot)
    return labels


def draw_corner_nodes(key, part):
    key = jax.random.fold_in(key, 11)

    def single(box_index):
        box_key = jax.random.fold_in(key, box_index)
        labels = spread_labels(box_key, NODES)[:NODES]
        element = jnp.arange(BOX_ELEMS)
        column_x = element // (BY * BZ)
        column_y = element // BZ % BY
        column_z = element % BZ
        corner = jnp.arange(8)[:, None]
        grid_index = ((column_x[None] + corner % 2) * (BY + 1) + column_y[None] + corner // 2 % 2) * (BZ + 1) + column_z[None] + corner // 4
        labeled = labels[grid_index]
        order = jax.random.permutation(jax.random.fold_in(box_key, 2), BOX_ELEMS)
        return labeled[:, order]
    stacked = jax.vmap(single)(jnp.arange(BOXES))
    return jnp.transpose(stacked, (1, 0, 2)).astype(jnp.int32)


def draw_live_counts(key, part):
    key = jax.random.fold_in(key, 13)
    members = BOX_ELEMS // E_DEV
    counts = jax.random.randint(jax.random.fold_in(key, 1), (BOXES * members,), E_DEV // 4, E_DEV + 1)
    picks = jax.random.permutation(jax.random.fold_in(key, 2), BOXES * members)
    counts = counts.at[picks[0]].set(E_DEV).at[picks[1]].set(E_DEV // 4)
    return counts.reshape(BOXES, members).astype(jnp.int32)


def draw_layer_nodes(key, part):
    key = jax.random.fold_in(key, 17)

    def single(box_index):
        return spread_labels(jax.random.fold_in(key, box_index), LAYER)[:LAYER]
    return jax.vmap(single)(jnp.arange(BOXES)).astype(jnp.int32)


def place_ends(array, own_key, least, largest):
    longest = array.shape.index(max(array.shape))
    spots = []
    for shift in (0, 1):
        where = [jax.random.randint(jax.random.fold_in(own_key, axis), (), 0, length) for axis, length in enumerate(array.shape)]
        where[longest] = (where[longest] + shift) % array.shape[longest]
        spots.append(tuple(where))
    return array.at[spots[0]].set(least).at[spots[1]].set(largest)


def block_levels(rng, dims, split, least, high):
    loudness = 1.0
    for position, shards_of in split:
        draws = jax.random.uniform(jax.random.fold_in(jax.random.fold_in(rng, 6), position), (shards_of,), jnp.float32, least / len(split), high / len(split))
        loudness = loudness * jnp.repeat(jnp.exp(draws), dims[position] // shards_of).reshape((-1,) + (1,) * (len(dims) - 1 - position))
    return loudness


def shared_out(own_key, own, number, rows, number_of, top, limit, lean):
    ranking = jax.random.permutation(own_key, number_of)
    crowded, ordinary = load_shares(number_of, rows * top, limit, lean, True), load_shares(number_of, rows * top, limit, lean, False)
    places = jnp.arange(number_of)

    def named(lengths, offset_by):
        used = int((lengths > 0).sum())
        fixed = max(1, used // 4)
        moved = fixed + (places - fixed + offset_by * (used - fixed)) % max(1, number_of - fixed)
        return jnp.zeros((number_of,), jnp.int32).at[ranking[jnp.where(places < fixed, places, moved)]].set(jnp.asarray(lengths, jnp.int32))

    lengths = jnp.where(number % 4 == 0, named(crowded, number // 4), named(ordinary, number - number // 4 - 1))
    mixed = jax.random.permutation(jax.random.fold_in(own, 3), number_of)
    giver, receiver = mixed[0:number_of // 2 * 2:2], mixed[1:number_of // 2 * 2:2]
    slack = jnp.minimum(lengths[giver] - 1, limit - lengths[receiver]) // 2
    slack = jnp.where((giver == ranking[0]) | (receiver == ranking[0]) | (lengths[receiver] == 0), 0, jnp.maximum(slack, 0))
    moved = jax.random.randint(jax.random.fold_in(own, 4), (number_of // 2,), 0, 1 << 20) % (slack + 1)
    lengths = lengths.at[giver].add(-moved).at[receiver].add(moved)
    items = jnp.searchsorted(jnp.cumsum(lengths), jnp.arange(rows * top), side="right").astype(jnp.int32)
    table = items.reshape(top, rows).T
    table = table[jax.random.permutation(jax.random.fold_in(own, 1), rows)]
    offset_by = jax.random.randint(jax.random.fold_in(own, 2), (rows, 1), 0, top)
    return jnp.take_along_axis(table, (jnp.arange(top)[None, :] + offset_by) % top, axis=1)


def load_shares(amount, total, most, slope, full):
    portions = [(1 << 20) // math.isqrt(standing ** slope) + 1 for standing in range(1, amount + 1)]
    largest = most if full else min(most, max(-(-total // amount), total * portions[0] // sum(portions)))
    least = 1 if total - largest >= amount - 1 else 0
    given, rest = [largest] + [least] * (amount - 1), total - largest - least * (amount - 1)
    while rest > 0:
        free = [i for i in range(1, amount) if given[i] < largest] or [i for i in range(1, amount) if given[i] < most]
        whole, remaining = sum([portions[i] for i in free]), rest
        for i in free:
            more = min(most - given[i], max(1, remaining * portions[i] // whole), rest)
            given[i] = given[i] + more
            rest = rest - more
    return np.array(given)


def noise(key, shape, deviation, reach, pieces=(), kind=jnp.bfloat16):
    values = deviation * jax.random.normal(key, shape, jnp.float32)
    if pieces:
        values = values * block_levels(key, shape, pieces, -0.22, 0.18)
    return jnp.clip(values, -reach, reach).astype(kind)


def setup_inputs(seed: int = 0) -> dict:
    streams_of = jax.random.split(jax.random.key(seed), 15)
    grid_now = noise(streams_of[0], (3, NX, NY, NZ), 1.0, 6.0, ((1, 16), (2, 8)), jnp.float32)
    grid_before = noise(streams_of[1], (3, NX, NY, NZ), 1.0, 6.0, ((1, 16), (2, 8)), jnp.float32)
    wave_factor = jnp.clip(jnp.exp(math.log(0.2) - 1.609438 * jax.random.uniform(streams_of[2], (NX, NY, NZ), jnp.float32) ** block_levels(streams_of[2], (NX, NY, NZ), ((0, 16), (1, 8)), -0.2, 0.2)), 0.04, 0.2)
    layer_owner_keys = jax.random.split(jax.random.fold_in(streams_of[3], 1), BOXES * LAYER // LAYER_DEV)
    layer_owner_turns = jax.random.permutation(jax.random.fold_in(streams_of[3], 3), BOXES * LAYER // LAYER_DEV)
    layer_owner = jax.vmap(lambda own, number: shared_out(jax.random.fold_in(streams_of[3], 2), own, number, LAYER_DEV, DEVICES, 1, CAP, 1))(layer_owner_keys, layer_owner_turns).reshape((BOXES, LAYER, 1))
    layer_cell = place_ends(jax.random.randint(streams_of[4], (BOXES, LAYER), 0, CELLS_DEV), jax.random.fold_in(streams_of[4], 1), 0, CELLS_DEV - 1).astype(jnp.int32)
    box_now = noise(streams_of[5], (3, BOXES, BOX_NODES), 1.0, 6.0, ((1, 16), (2, 8)), jnp.float32)
    box_before = noise(streams_of[6], (3, BOXES, BOX_NODES), 1.0, 6.0, ((1, 16), (2, 8)), jnp.float32)
    node_mass = jnp.clip(jnp.exp(math.log(2.0) - 1.3862944 * jax.random.uniform(streams_of[7], (BOXES, BOX_NODES), jnp.float32) ** block_levels(streams_of[7], (BOXES, BOX_NODES), ((0, 16), (1, 8)), -0.2, 0.2)), 0.5, 2.0)
    corner_nodes = draw_corner_nodes(jax.random.fold_in(streams_of[14], 71), 0)
    live_counts = draw_live_counts(jax.random.fold_in(streams_of[14], 71), 0)
    shear_modulus = jnp.clip(jnp.exp(math.log(2.0) - 2.0794415 * jax.random.uniform(streams_of[10], (BOXES, BOX_ELEMS), jnp.float32) ** block_levels(streams_of[10], (BOXES, BOX_ELEMS), ((0, 16), (1, 8)), -0.2, 0.2)), 0.25, 2.0)
    lame_lambda = jnp.clip(jnp.exp(math.log(4.0) - 2.0794415 * jax.random.uniform(streams_of[11], (BOXES, BOX_ELEMS), jnp.float32) ** block_levels(streams_of[11], (BOXES, BOX_ELEMS), ((0, 16), (1, 8)), -0.2, 0.2)), 0.5, 4.0)
    strain_scale = jnp.clip(jnp.exp(math.log(2.0) - 2.3025851 * jax.random.uniform(streams_of[12], (BOXES, BOX_ELEMS), jnp.float32) ** block_levels(streams_of[12], (BOXES, BOX_ELEMS), ((0, 16), (1, 8)), -0.2, 0.2)), 0.2, 2.0)
    layer_nodes = draw_layer_nodes(jax.random.fold_in(streams_of[14], 71), 0)
    return dict(grid_now=grid_now, grid_before=grid_before, wave_factor=wave_factor, layer_owner=layer_owner, layer_cell=layer_cell, box_now=box_now, box_before=box_before, node_mass=node_mass, corner_nodes=corner_nodes, live_counts=live_counts, shear_modulus=shear_modulus, lame_lambda=lame_lambda, strain_scale=strain_scale, layer_nodes=layer_nodes)


PENALTY = 2.0
STEP_SQUARE = 0.25


def stencil(extended, row_count, col_count):
    padded = jnp.pad(extended, ((0, 0), (0, 0), (0, 0), (2, 2)))
    channels = extended.shape[0]
    extent = extended.shape[3]

    def shifted(along_x, along_y, along_z):
        return lax.slice(padded, (0, 2 + along_x, 2 + along_y, 2 + along_z),
                         (channels, 2 + along_x + row_count, 2 + along_y + col_count, 2 + along_z + extent))

    result = -7.5 * shifted(0, 0, 0)
    for offset, weight in ((1, 16.0 / 12.0), (2, -1.0 / 12.0)):
        for orient in (1, -1):
            result = result + weight * (shifted(orient * offset, 0, 0) + shifted(0, orient * offset, 0)
                                        + shifted(0, 0, orient * offset))
    return result


def corner_gradients():
    corner = jnp.arange(8)
    bit_rows = jnp.stack([(corner // (2 ** level)) % 2 for level in range(3)])
    return (2.0 * bit_rows.astype(jnp.float32) - 1.0) * 0.25


def element_forces(corner_disp, shear, lame, scale, weights):
    gradients = corner_gradients()
    disp_grad = jnp.einsum('ja,iae->ije', gradients, corner_disp, precision=lax.Precision.HIGHEST)
    strain = 0.5 * (disp_grad + jnp.transpose(disp_grad, (1, 0, 2)))
    trace = strain[0, 0] + strain[1, 1] + strain[2, 2]
    identity = jnp.eye(3, dtype=jnp.float32)[:, :, None]
    deviator = strain - identity * (trace / 3.0)
    invariant = jnp.sum(deviator * deviator, axis=(0, 1))
    softened = shear / (1.0 + invariant / scale)
    stress = (identity * (lame * trace) + 2.0 * softened * strain) * weights
    return jnp.einsum('ja,ije->iae', gradients, stress, precision=lax.Precision.HIGHEST)


def reference(grid_now, grid_before, wave_factor, layer_owner, layer_cell, box_now, box_before,
              node_mass, corner_nodes, live_counts, shear_modulus, lame_lambda, strain_scale, layer_nodes):
    factor = wave_factor[None]

    def advance(current, previous):
        padded = jnp.pad(current, ((0, 0), (2, 2), (2, 2), (0, 0)))
        return 2.0 * current - previous + factor * stencil(padded, NX, NY)

    grid_mid = advance(grid_now, grid_before)
    grid_after = advance(grid_mid, grid_now)

    owners = layer_owner[:, :, 0]
    first_index = (owners // N_GY) * CX + layer_cell // (CY * NZ)
    second_index = (owners % N_GY) * CY + (layer_cell // NZ) % CY
    third_index = layer_cell % NZ
    motion = grid_after[:, first_index, second_index, third_index]

    def one_box(bundle):
        disp, previous, corners, counts, shear, lame, scale, mass, layer_ids, layer_motion = bundle
        slot_index = jnp.arange(BOX_ELEMS)
        weights = (slot_index % E_DEV < counts[slot_index // E_DEV]).astype(jnp.float32)
        corner_disp = disp[:, corners]
        forces = element_forces(corner_disp, shear, lame, scale, weights)
        internal = jnp.zeros((3, BOX_NODES), jnp.float32).at[:, corners.reshape(-1)].add(forces.reshape(3, -1))
        coupling = jnp.zeros((3, BOX_NODES), jnp.float32).at[:, layer_ids].add(
            PENALTY * (layer_motion - disp[:, layer_ids]))
        return 2.0 * disp - previous + STEP_SQUARE / mass[None, :] * (coupling - internal)

    bundles = (jnp.transpose(box_now, (1, 0, 2)), jnp.transpose(box_before, (1, 0, 2)),
               jnp.transpose(corner_nodes, (1, 0, 2)), live_counts, shear_modulus, lame_lambda,
               strain_scale, node_mass, layer_nodes, jnp.transpose(motion, (1, 0, 2)))
    box_after = jnp.transpose(lax.map(one_box, bundles), (1, 0, 2))
    return grid_after, box_after
```

```python
import functools

import jax
import jax.numpy as jnp
from jax import lax
from jax.experimental import pallas as pl
from jax.experimental.pallas import tpu as pltpu
from jax.sharding import PartitionSpec as P

PENALTY = 2.0
STEP_SQUARE = 0.25
LANES = 128
SLOTS = 16
VMEM_LIMIT = 56 * 2**20
GATHER_UNROLL = 8
SCATTER_UNROLL = 16
LAYER_UNROLL = 16


def gradient_signs(corner):
    lane = lax.broadcasted_iota(jnp.int32, (1, LANES), 1)
    signs = jnp.zeros((1, LANES), jnp.float32)
    for direction in range(3):
        value = 0.25 if (corner >> direction) & 1 else -0.25
        inside = (lane >= 3 * direction) & (lane < 3 * direction + 3)
        signs = jnp.where(inside, value, signs)
    return signs


def rows_of(values):
    count = values.shape[0]
    padded = jnp.concatenate(
        [values, jnp.zeros((SLOTS - count, LANES), jnp.float32)], axis=0
    )
    return padded.T


def aligned(start):
    return pl.multiple_of(start, LANES)


def gather_kernel(
    live_ref, layer_ref, corner_hbm, disp_ref, shear_ref, lame_ref, scale_ref,
    stress_ref, layer_out, table, grad_rows, layer_rows, *rest,
):
    ids, sems = rest[:8], rest[8]
    copies = [
        pltpu.make_async_copy(corner_hbm.at[corner, 0], ids[corner], sems.at[corner])
        for corner in range(8)
    ]
    for copy in copies:
        copy.start()
    owners, _, own = disp_ref.shape

    def build(part, carry):
        for tile in range(own // LANES):
            block = disp_ref[part, :, tile * LANES : (tile + 1) * LANES]
            rows = rows_of(jnp.concatenate([block, block, block], axis=0))
            table[pl.ds(aligned(part * own + tile * LANES), LANES), 0:SLOTS] = rows
        return carry

    lax.fori_loop(0, owners, build, 0)
    for copy in copies:
        copy.wait()
    signs = [gradient_signs(corner) for corner in range(4)]
    live = live_ref[0, 0]

    def gather(chunk, carry):
        base = chunk * GATHER_UNROLL
        for step in range(GATHER_UNROLL):
            slot = base + step
            rows = [table[pl.ds(ids[corner][slot], 1), :] for corner in range(8)]
            spans = [rows[corner] - rows[7 - corner] for corner in range(4)]
            grad_rows[pl.ds(slot, 1), :] = (spans[0] * signs[0] + spans[1] * signs[1]) + (
                spans[2] * signs[2] + spans[3] * signs[3]
            )
        return carry

    lax.fori_loop(0, (live + GATHER_UNROLL - 1) // GATHER_UNROLL, gather, 0)

    def layer(chunk, carry):
        base = chunk * LAYER_UNROLL
        for step in range(LAYER_UNROLL):
            node = layer_ref[0, base + step]
            layer_rows[pl.ds(base + step, 1), :] = table[pl.ds(node, 1), :]
        return carry

    lax.fori_loop(0, layer_rows.shape[0] // LAYER_UNROLL, layer, 0)
    for tile in range(layer_rows.shape[0] // LANES):
        block = layer_rows[tile * LANES : (tile + 1) * LANES, 0:SLOTS].T
        layer_out[:, tile * LANES : (tile + 1) * LANES] = block[0:3] * -PENALTY

    def element(tile, carry):
        start = aligned(tile * LANES)
        grads = grad_rows[pl.ds(start, LANES), 0:SLOTS].T
        slope = [[grads[3 * j + i : 3 * j + i + 1] for j in range(3)] for i in range(3)]
        s00, s11, s22 = slope[0][0], slope[1][1], slope[2][2]
        s01 = 0.5 * (slope[0][1] + slope[1][0])
        s02 = 0.5 * (slope[0][2] + slope[2][0])
        s12 = 0.5 * (slope[1][2] + slope[2][1])
        trace = s00 + s11 + s22
        mean = trace / 3.0
        d00, d11, d22 = s00 - mean, s11 - mean, s22 - mean
        invariant = d00 * d00 + d11 * d11 + d22 * d22
        invariant = invariant + 2.0 * (s01 * s01 + s02 * s02 + s12 * s12)
        here = pl.ds(start, LANES)
        softened = 2.0 * shear_ref[:, here] / (1.0 + invariant / scale_ref[:, here])
        volume = lame_ref[:, here] * trace
        index = start + lax.broadcasted_iota(jnp.int32, (1, LANES), 1)

        def signed(value):
            return jnp.where(index < live, -value, 0.0)

        p00 = signed(volume + softened * s00)
        p11 = signed(volume + softened * s11)
        p22 = signed(volume + softened * s22)
        p01, p02, p12 = signed(softened * s01), signed(softened * s02), signed(softened * s12)
        stress_ref[tile] = jnp.concatenate(
            [p00, p01, p02, p01, p11, p12, p02, p12, p22, jnp.zeros((7, LANES), jnp.float32)],
            axis=0,
        )
        return carry

    lax.fori_loop(0, stress_ref.shape[0], element, 0)


def scatter_kernel(
    live_ref, layer_ref, slot_ref, corner_hbm, stress_ref, layer_in, reply_ref,
    out_ref, total, stress_rows, layer_rows, reply_rows, *rest,
):
    ids, sems = rest[:8], rest[8]
    copies = [
        pltpu.make_async_copy(corner_hbm.at[corner, 0], ids[corner], sems.at[corner])
        for corner in range(8)
    ]
    for copy in copies:
        copy.start()
    owners, _, own = out_ref.shape

    def clear(chunk, carry):
        zero = jnp.zeros((LANES, LANES), jnp.float32)
        total[pl.ds(aligned(chunk * LANES), LANES), :] = zero
        return carry

    lax.fori_loop(0, total.shape[0] // LANES, clear, 0)

    def to_rows(tile, carry):
        stress_rows[pl.ds(aligned(tile * LANES), LANES), 0:SLOTS] = stress_ref[tile].T
        return carry

    lax.fori_loop(0, stress_ref.shape[0], to_rows, 0)
    for tile in range(layer_rows.shape[0] // LANES):
        here = slice(tile * LANES, (tile + 1) * LANES)
        layer_rows[here, 0:SLOTS] = rows_of(layer_in[:, here])
    for tile in range(reply_rows.shape[0] // LANES):
        here = slice(tile * LANES, (tile + 1) * LANES)
        reply_rows[here, 0:SLOTS] = rows_of(reply_ref[:, here] * PENALTY)
    for copy in copies:
        copy.wait()
    signs = [gradient_signs(corner) for corner in range(8)]
    live = live_ref[0, 0]

    def scatter(chunk, carry):
        base = chunk * SCATTER_UNROLL
        steps = range(SCATTER_UNROLL)
        rows = [stress_rows[pl.ds(base + step, 1), :] for step in steps]
        for corner in range(8):
            nodes = [ids[corner][base + step] for step in steps]
            held = [total[pl.ds(nodes[step], 1), :] for step in steps]
            held = [held[step] + rows[step] * signs[corner] for step in steps]
            for step in steps:
                total[pl.ds(nodes[step], 1), :] = held[step]
        return carry

    lax.fori_loop(0, (live + SCATTER_UNROLL - 1) // SCATTER_UNROLL, scatter, 0)

    def layer(chunk, carry):
        base = chunk * LAYER_UNROLL
        steps = range(LAYER_UNROLL)
        nodes = [layer_ref[0, base + step] for step in steps]
        held = [total[pl.ds(nodes[step], 1), :] for step in steps]
        for step in steps:
            reply = reply_rows[pl.ds(slot_ref[0, base + step], 1), :]
            held[step] = held[step] + (reply + layer_rows[pl.ds(base + step, 1), :])
        for step in steps:
            total[pl.ds(nodes[step], 1), :] = held[step]
        return carry

    lax.fori_loop(0, layer_rows.shape[0] // LAYER_UNROLL, layer, 0)

    def fold(part, carry):
        for tile in range(own // LANES):
            start = aligned(part * own + tile * LANES)
            block = total[pl.ds(start, LANES), 0:SLOTS].T
            out_ref[part, :, tile * LANES : (tile + 1) * LANES] = (
                block[0:3] + block[3:6] + block[6:9]
            )
        return carry

    lax.fori_loop(0, owners, fold, 0)


def in_smem():
    return pl.BlockSpec(memory_space=pltpu.SMEM)


def in_vmem():
    return pl.BlockSpec(memory_space=pltpu.VMEM)


def in_any():
    return pl.BlockSpec(memory_space=pl.ANY)


def gather_elements(live, layer_ids, corner_ids, disp, shear, lame, scale):
    owners, _, own = disp.shape
    slots = corner_ids.shape[2]
    layers = layer_ids.shape[1]
    return pl.pallas_call(
        gather_kernel,
        out_shape=(
            jax.ShapeDtypeStruct((slots // LANES, SLOTS, LANES), jnp.float32),
            jax.ShapeDtypeStruct((3, layers), jnp.float32),
        ),
        in_specs=[in_smem(), in_smem(), in_any()] + [in_vmem()] * 4,
        out_specs=(in_vmem(), in_vmem()),
        scratch_shapes=[
            pltpu.VMEM((owners * own, LANES), jnp.float32),
            pltpu.VMEM((slots, LANES), jnp.float32),
            pltpu.VMEM((layers, LANES), jnp.float32),
        ]
        + [pltpu.SMEM((slots,), jnp.int32)] * 8
        + [pltpu.SemaphoreType.DMA((8,))],
        compiler_params=pltpu.CompilerParams(vmem_limit_bytes=VMEM_LIMIT),
        cost_estimate=pl.CostEstimate(
            flops=200_000_000, bytes_accessed=180_000_000, transcendentals=0
        ),
        name="corner_gather",
    )(live, layer_ids, corner_ids, disp, shear, lame, scale)


def scatter_forces(live, layer_ids, slot_index, corner_ids, stress, layer_term, replies, owners, own):
    slots = corner_ids.shape[2]
    layers = layer_ids.shape[1]
    return pl.pallas_call(
        scatter_kernel,
        out_shape=jax.ShapeDtypeStruct((owners, 3, own), jnp.float32),
        in_specs=[in_smem(), in_smem(), in_smem(), in_any()] + [in_vmem()] * 3,
        out_specs=in_vmem(),
        scratch_shapes=[
            pltpu.VMEM((owners * own, LANES), jnp.float32),
            pltpu.VMEM((slots, LANES), jnp.float32),
            pltpu.VMEM((layers, LANES), jnp.float32),
            pltpu.VMEM((replies.shape[1], LANES), jnp.float32),
        ]
        + [pltpu.SMEM((slots,), jnp.int32)] * 8
        + [pltpu.SemaphoreType.DMA((8,))],
        compiler_params=pltpu.CompilerParams(vmem_limit_bytes=VMEM_LIMIT),
        cost_estimate=pl.CostEstimate(
            flops=200_000_000, bytes_accessed=250_000_000, transcendentals=0
        ),
        name="force_scatter",
    )(live, layer_ids, slot_index, corner_ids, stress, layer_term, replies)


def stencil_kernel(now, before, factor, x_low, x_high, y_low, y_high, out):
    planes, rows, cols = now.shape[1:]

    def plane(index):
        if index < 0:
            return x_low[0, index + 2]
        if index >= planes:
            return x_high[0, index - planes]
        return now[0, index]

    row = lax.broadcasted_iota(jnp.int32, (rows, cols), 0)
    col = lax.broadcasted_iota(jnp.int32, (rows, cols), 1)
    for index in range(planes):
        here = plane(index)
        low, high = y_low[0, index], y_high[0, index]
        down1 = jnp.where(row == 0, low[1:2], pltpu.roll(here, 1, 0))
        down2 = jnp.where(row == 0, low[0:1], jnp.where(row == 1, low[1:2], pltpu.roll(here, 2, 0)))
        up1 = jnp.where(row == rows - 1, high[0:1], pltpu.roll(here, rows - 1, 0))
        up2 = jnp.where(
            row == rows - 1,
            high[1:2],
            jnp.where(row == rows - 2, high[0:1], pltpu.roll(here, rows - 2, 0)),
        )
        left1 = jnp.where(col == 0, 0.0, pltpu.roll(here, 1, 1))
        left2 = jnp.where(col < 2, 0.0, pltpu.roll(here, 2, 1))
        right1 = jnp.where(col == cols - 1, 0.0, pltpu.roll(here, cols - 1, 1))
        right2 = jnp.where(col >= cols - 2, 0.0, pltpu.roll(here, cols - 2, 1))
        near = (plane(index - 1) + plane(index + 1)) + (down1 + up1) + (left1 + right1)
        far = (plane(index - 2) + plane(index + 2)) + (down2 + up2) + (left2 + right2)
        laplace = (16.0 / 12.0) * near - (1.0 / 12.0) * far - 7.5 * here
        out[0, index] = 2.0 * here - before[0, index] + factor[index] * laplace


def advance(now, before, factor, halos):
    comps, planes, rows, cols = now.shape
    block = pl.BlockSpec((1, planes, rows, cols), lambda c: (c, 0, 0, 0))
    x_side = pl.BlockSpec((1, 2, rows, cols), lambda c: (c, 0, 0, 0))
    y_side = pl.BlockSpec((1, planes, 2, cols), lambda c: (c, 0, 0, 0))
    return pl.pallas_call(
        stencil_kernel,
        grid=(comps,),
        out_shape=jax.ShapeDtypeStruct(now.shape, jnp.float32),
        in_specs=[
            block,
            block,
            pl.BlockSpec((planes, rows, cols), lambda c: (0, 0, 0)),
            x_side,
            x_side,
            y_side,
            y_side,
        ],
        out_specs=block,
        compiler_params=pltpu.CompilerParams(vmem_limit_bytes=VMEM_LIMIT),
        cost_estimate=pl.CostEstimate(
            flops=30_000_000, bytes_accessed=30_000_000, transcendentals=0
        ),
        name="wave_step",
    )(now, before, factor, *halos)


def exchange(field):
    halos = []
    for axis, dim in (("gx", 1), ("gy", 2)):
        count = lax.axis_size(axis)
        forward = [(i, i + 1) for i in range(count - 1)]
        backward = [(target, source) for source, target in forward]
        last = lax.slice_in_dim(field, field.shape[dim] - 2, None, axis=dim)
        first = lax.slice_in_dim(field, 0, 2, axis=dim)
        halos += [lax.ppermute(last, axis, forward), lax.ppermute(first, axis, backward)]
    return halos


def motion_kernel(wanted, field, out):
    lane = lax.broadcasted_iota(jnp.int32, (1, LANES), 1)

    def group(part, carry):
        def step(chunk, held):
            held = list(held)
            for inner in range(8):
                position = chunk * 8 + inner
                cell = wanted[part * LANES + position]
                row = cell >> 7
                shift = (position - cell) & (LANES - 1)
                for comp in range(3):
                    values = field[comp, pl.ds(row, 1), :]
                    held[comp] = jnp.where(
                        lane == position, pltpu.roll(values, shift, 1), held[comp]
                    )
            return tuple(held)

        zero = jnp.zeros((1, LANES), jnp.float32)
        held = lax.fori_loop(0, LANES // 8, step, (zero, zero, zero))
        for comp in range(3):
            out[part, pl.ds(comp, 1), :] = held[comp]
        return carry

    lax.fori_loop(0, out.shape[0], group, 0)


def gather_motion(wanted, field):
    count = wanted.shape[0]
    comps, planes, rows, cols = field.shape
    tiles = field.reshape(comps, planes, rows // 8, 8, cols // LANES, LANES)
    field = jnp.transpose(tiles, (0, 1, 2, 4, 3, 5)).reshape(comps, -1, LANES)
    plane, row, col = wanted // (rows * cols), wanted // cols % rows, wanted % cols
    tile = (plane * (rows // 8) + row // 8) * (cols // LANES) + col // LANES
    wanted = (tile * 8 + row % 8) * LANES + col % LANES
    return pl.pallas_call(
        motion_kernel,
        out_shape=jax.ShapeDtypeStruct((count // LANES, 3, LANES), jnp.float32),
        in_specs=[in_smem(), in_vmem()],
        out_specs=in_vmem(),
        compiler_params=pltpu.CompilerParams(vmem_limit_bytes=VMEM_LIMIT),
        name="motion_gather",
    )(wanted, field)


def on_device(
    grid_now,
    grid_before,
    wave_factor,
    layer_owner,
    layer_cell,
    box_now,
    box_before,
    node_mass,
    corner_nodes,
    live_counts,
    shear_modulus,
    lame_lambda,
    strain_scale,
    layer_nodes,
):
    own_disp = box_now.reshape(3, -1)
    own = own_disp.shape[1]
    all_disp = lax.all_gather(own_disp, "gy", axis=0, tiled=False)
    first_halos = exchange(grid_now)

    owners = layer_owner.reshape(-1)
    cell_index = layer_cell.reshape(-1)
    count_gx = lax.axis_size("gx")
    count_gy = lax.axis_size("gy")
    devices = count_gx * count_gy
    capacity = 2 * owners.shape[0] // devices
    rank_rows = jnp.arange(owners.shape[0])
    earlier = (rank_rows[None, :] < rank_rows[:, None]).astype(jnp.bfloat16)
    matches = owners[:, None] == jnp.arange(devices)[None, :]
    before = jnp.dot(earlier, matches.astype(jnp.bfloat16), preferred_element_type=jnp.float32)
    position = jnp.sum(jnp.where(matches, before, 0.0), axis=1).astype(jnp.int32)
    slot_index = owners * capacity + position
    requests = (
        jnp.zeros((devices * capacity,), jnp.int32)
        .at[slot_index]
        .set(cell_index, unique_indices=True)
    )
    wanted = lax.all_to_all(
        requests.reshape(devices, capacity), ("gx", "gy"), split_axis=0, concat_axis=0, tiled=True
    )

    grid_mid = advance(grid_now, grid_before, wave_factor, first_halos)
    second_halos = exchange(grid_mid)
    stress, layer_term = gather_elements(
        live_counts, layer_nodes, corner_nodes, all_disp, shear_modulus, lame_lambda, strain_scale
    )
    grid_after = advance(grid_mid, grid_now, wave_factor, second_halos)
    moved = gather_motion(wanted.reshape(-1), grid_after)
    moved = jnp.transpose(moved, (1, 0, 2)).reshape(3, devices, capacity)
    returned = lax.all_to_all(moved, ("gx", "gy"), split_axis=1, concat_axis=1, tiled=True)
    node_term = scatter_forces(
        live_counts,
        layer_nodes,
        slot_index.reshape(1, -1),
        corner_nodes,
        stress,
        layer_term,
        returned.reshape(3, devices * capacity),
        count_gy,
        own,
    )
    parts = lax.all_to_all(node_term, "gy", split_axis=0, concat_axis=0, tiled=True)
    summed = jnp.sum(parts, axis=0)
    box_after = 2.0 * own_disp - box_before.reshape(3, -1) + STEP_SQUARE / node_mass * summed
    return (grid_after, box_after.reshape(box_now.shape))


def solution(mesh):
    return jax.shard_map(
        on_device,
        mesh=mesh,
        in_specs=(
            P(None, "gx", "gy", None),
            P(None, "gx", "gy", None),
            P("gx", "gy", None),
            P("gx", "gy", None),
            P("gx", "gy"),
            P(None, "gx", "gy"),
            P(None, "gx", "gy"),
            P("gx", "gy"),
            P(None, "gx", "gy"),
            P("gx", "gy"),
            P("gx", "gy"),
            P("gx", "gy"),
            P("gx", "gy"),
            P("gx", "gy"),
        ),
        out_specs=(P(None, "gx", "gy", None), P(None, "gx", "gy")),
        check_vma=False,
    )
```

```python
import jax
import jax.numpy as jnp
from jax import lax
from jax.experimental import pallas as pl
from jax.experimental.pallas import tpu as pltpu
from jax.sharding import PartitionSpec as P

PENALTY = 2.0
STEP_SQUARE = 0.25
NEAR = 16.0 / 12.0
FAR = -1.0 / 12.0
LANES = 128
SLOTS = 16
ID_ROWS = 72
PLANE = 128
VMEM_LIMIT = 58 * 2**20
GATHER_UNROLL = 16
SCATTER_UNROLL = 2
LAYER_UNROLL = 16
MESH = pl.DeviceIdType.MESH


def aligned(start, unit=LANES):
    return pl.multiple_of(start, unit)


def wave_plane(comp, index, now, before, factor, out, out_shift):
    start = aligned((index + 2) * PLANE)

    def block(offset, group, tile):
        return now[comp, pl.ds(start + offset * PLANE + (group * 4 + tile) * 8, 8), :]

    sub = lax.broadcasted_iota(jnp.int32, (8, LANES), 0)
    lane = lax.broadcasted_iota(jnp.int32, (8, LANES), 1)
    zero = jnp.zeros((8, LANES), jnp.float32)
    here = [[block(0, group, tile) for tile in range(4)] for group in range(4)]

    def neighbours(values, axis, count, position):
        sums = []
        for distance in (1, 2):
            ahead = [pltpu.roll(value, distance, axis) for value in values]
            behind = [pltpu.roll(value, count - distance, axis) for value in values]
            rows = []
            for spot in range(4):
                low = ahead[spot - 1] if spot > 0 else zero
                high = behind[spot + 1] if spot < 3 else zero
                rows.append(
                    jnp.where(position < distance, low, ahead[spot])
                    + jnp.where(position >= count - distance, high, behind[spot])
                )
            sums.append(rows)
        return sums

    along_y = [neighbours([here[g][t] for g in range(4)], 0, 8, sub) for t in range(4)]
    along_z = [neighbours(here[g], 1, LANES, lane) for g in range(4)]
    for group in range(4):
        for tile in range(4):
            row = (group * 4 + tile) * 8
            near = block(-1, group, tile) + block(1, group, tile)
            far = block(-2, group, tile) + block(2, group, tile)
            near = near + (along_y[tile][0][group] + along_z[group][0][tile])
            far = far + (along_y[tile][1][group] + along_z[group][1][tile])
            centre = here[group][tile]
            laplace = NEAR * near + FAR * far - 7.5 * centre
            place = pl.ds(aligned(index * PLANE) + row, 8)
            result = 2.0 * centre - before[comp, pl.ds(aligned(before_start(before, index)) + row, 8), :]
            out[comp, pl.ds(aligned((index + out_shift) * PLANE) + row, 8), :] = (
                result + factor[place, :] * laplace
            )


def before_start(before, index):
    shift = 2 if before.shape[1] == 20 * PLANE else 0
    return (index + shift) * PLANE


def y_edges(comp, index, source, low_out, high_out):
    start = aligned((index + 2) * PLANE)
    for tile in range(4):
        first = source[comp, pl.ds(start + tile * 8, 8), :]
        last = source[comp, pl.ds(start + 96 + tile * 8, 8), :]
        low_out[comp, index, 2 * tile : 2 * tile + 2, :] = first[0:2]
        high_out[comp, index, 2 * tile : 2 * tile + 2, :] = last[6:8]


def y_corrections(comp, index, low, high, low_weight, high_weight, factor, out, out_shift):
    sub = lax.broadcasted_iota(jnp.int32, (8, LANES), 0)
    start = aligned((index + out_shift) * PLANE)
    here = aligned(index * PLANE)
    lows = low[comp, index] * low_weight
    highs = high[comp, index] * high_weight
    for tile in range(4):
        far_row, near_row = lows[2 * tile : 2 * tile + 1], lows[2 * tile + 1 : 2 * tile + 2]
        term = jnp.where(
            sub == 0, NEAR * near_row + FAR * far_row, jnp.where(sub == 1, FAR * near_row, 0.0)
        )
        place = pl.ds(start + tile * 8, 8)
        out[comp, place, :] = out[comp, place, :] + factor[pl.ds(here + tile * 8, 8), :] * term
        near_row, far_row = highs[2 * tile : 2 * tile + 1], highs[2 * tile + 1 : 2 * tile + 2]
        term = jnp.where(
            sub == 7, NEAR * near_row + FAR * far_row, jnp.where(sub == 6, FAR * near_row, 0.0)
        )
        place = pl.ds(start + 96 + tile * 8, 8)
        out[comp, place, :] = out[comp, place, :] + factor[pl.ds(here + 96 + tile * 8, 8), :] * term


def grid_kernel(
    now_hbm, before_hbm, factor_hbm, request, disp_hbm, ids_hbm, params_hbm,
    after_hbm, disp_all, ids_all, params_all, reply_out,
    now, mid, after, before, factor, y_sent, y_got, asked_x, asked_t, asked_y, rows_vmem,
    rows_smem, found, found_x, found_t, send_sems, recv_sems, local_sems,
):
    gx, gy = lax.axis_index("gx"), lax.axis_index("gy")
    count_x, count_y = lax.axis_size("gx"), lax.axis_size("gy")
    planes = factor.shape[0] // PLANE
    edge = 2 * PLANE
    inside = pl.ds(edge, planes * PLANE)

    loads = [
        pltpu.make_async_copy(now_hbm, now.at[:, inside, :], local_sems.at[0]),
        pltpu.make_async_copy(before_hbm, before, local_sems.at[1]),
        pltpu.make_async_copy(factor_hbm, factor, local_sems.at[2]),
    ]
    for load in loads:
        load.start()

    barrier = pltpu.get_barrier_semaphore()
    for step in range(1, count_x):
        peer = lax.rem(gx + step, count_x)
        pl.semaphore_signal(barrier, inc=1, device_id=(peer, gy), device_id_type=MESH)
    for step in range(1, count_y):
        peer = lax.rem(gy + step, count_y)
        pl.semaphore_signal(barrier, inc=1, device_id=(gx, peer), device_id_type=MESH)
    pl.semaphore_wait(barrier, count_x + count_y - 2)

    used = [0]

    def send(source, target, device):
        slot = used[0]
        used[0] += 1
        copy = pltpu.make_async_remote_copy(
            src_ref=source,
            dst_ref=target,
            send_sem=send_sems.at[slot],
            recv_sem=recv_sems.at[slot],
            device_id=device,
            device_id_type=MESH,
        )
        copy.start()
        return copy

    right, left = lax.rem(gx + 1, count_x), lax.rem(gx + count_x - 1, count_x)
    upper, lower = lax.rem(gy + 1, count_y), lax.rem(gy + count_y - 1, count_y)
    top = (planes - 2) * PLANE

    def x_halo(source, shift, target):
        return [
            send(
                source.at[:, pl.ds(top + shift, edge), :],
                target.at[:, pl.ds(0, edge), :],
                (right, gy),
            ),
            send(
                source.at[:, pl.ds(shift, edge), :],
                target.at[:, pl.ds(edge + planes * PLANE, edge), :],
                (left, gy),
            ),
        ]

    def y_halo(step):
        return [
            send(y_sent.at[step, 1], y_got.at[step, 0], (gx, upper)),
            send(y_sent.at[step, 0], y_got.at[step, 1], (gx, lower)),
        ]

    def each_plane(indices, body):
        def run(comp, carry):
            for low, high in indices:
                lax.fori_loop(low, high, lambda index, c: (body(comp, index), c)[1], 0)
            return carry

        lax.fori_loop(0, 3, run, 0)

    def edges(step, source):
        each_plane(
            [(0, planes)],
            lambda comp, index: y_edges(comp, index, source, y_sent.at[step, 0], y_sent.at[step, 1]),
        )

    def clear_outside(target):
        @pl.when(gx == 0)
        def _():
            target[:, 0:edge, :] = jnp.zeros((3, edge, LANES), jnp.float32)

        @pl.when(gx == count_x - 1)
        def _():
            target[:, edge + planes * PLANE :, :] = jnp.zeros((3, edge, LANES), jnp.float32)

    low_weight = jnp.where(gy == 0, 0.0, 1.0).astype(jnp.float32)
    high_weight = jnp.where(gy == count_y - 1, 0.0, 1.0).astype(jnp.float32)

    first_x = x_halo(now_hbm, 0, now)
    asks = []
    for step in range(1, count_x):
        peer = lax.rem(gx + step, count_x)
        asks.append(send(request.at[peer], asked_x.at[gx], (peer, gy)))
    asked_x[gx] = request[gx]
    loads[0].wait()
    edges(0, now)
    first_y = y_halo(0)
    bulk = []
    for step in range(1, count_y):
        peer = lax.rem(gy + step, count_y)
        bulk.append(send(disp_hbm, disp_all.at[gy], (gx, peer)))
        bulk.append(send(ids_hbm.at[peer], ids_all.at[gy], (gx, peer)))
        bulk.append(send(params_hbm.at[peer], params_all.at[gy], (gx, peer)))
    own = [
        pltpu.make_async_copy(disp_hbm, disp_all.at[gy], local_sems.at[3]),
        pltpu.make_async_copy(ids_hbm.at[gy], ids_all.at[gy], local_sems.at[4]),
        pltpu.make_async_copy(params_hbm.at[gy], params_all.at[gy], local_sems.at[5]),
    ]
    for copy in own:
        copy.start()
    loads[1].wait()
    loads[2].wait()

    def step_of(source, previous, target, shift):
        return lambda comp, index: wave_plane(comp, index, source, previous, factor, target, shift)

    def fix(step, target, shift):
        each_plane(
            [(0, planes)],
            lambda comp, index: y_corrections(
                comp, index, y_got.at[step, 0], y_got.at[step, 1], low_weight, high_weight,
                factor, target, shift,
            ),
        )

    inner, outer = [(2, planes - 2)], [(0, 2), (planes - 2, planes)]
    first = step_of(now, before, mid, 2)
    each_plane(inner, first)
    for copy in asks:
        copy.wait()
    for peer in range(count_y):
        asked_t[peer] = asked_x[:, peer, :]
    passes = []
    for step in range(1, count_y):
        peer = lax.rem(gy + step, count_y)
        passes.append(send(asked_t.at[peer], asked_y.at[gy], (gx, peer)))
    asked_y[gy] = asked_t[gy]
    for copy in first_x:
        copy.wait()
    clear_outside(now)
    each_plane(outer, first)
    for copy in first_y:
        copy.wait()
    fix(0, mid, 2)

    second_x = x_halo(mid, edge, mid)
    edges(1, mid)
    second_y = y_halo(1)
    second = step_of(mid, now, after, 0)
    each_plane(inner, second)
    for copy in passes:
        copy.wait()
    cell = asked_y[...]
    plane, row, col = cell >> 14, (cell >> 9) & 31, cell & 511
    rows_vmem[...] = (((plane * 4 + (row >> 3)) * 4 + (col >> 7)) * 8 + (row & 7)) * LANES + (
        col & (LANES - 1)
    )
    to_smem = pltpu.make_async_copy(rows_vmem, rows_smem, local_sems.at[6])
    to_smem.start()
    for copy in second_x:
        copy.wait()
    clear_outside(mid)
    each_plane(outer, second)
    for copy in second_y:
        copy.wait()
    fix(1, after, 0)
    store = pltpu.make_async_copy(after, after_hbm, local_sems.at[7])
    store.start()
    to_smem.wait()

    lane = lax.broadcasted_iota(jnp.int32, (1, LANES), 1)
    capacity = LANES // SLOTS

    def find(source, carry):
        for part in range(count_y):
            held = jnp.zeros((1, LANES), jnp.float32)
            for position in range(capacity):
                place = rows_smem[part, source, position]
                line = place >> 7
                for comp in range(3):
                    spot = position * SLOTS + comp
                    values = after[comp, pl.ds(line, 1), :]
                    shift = (spot - place) & (LANES - 1)
                    held = jnp.where(lane == spot, pltpu.roll(values, shift, 1), held)
            found[part, pl.ds(source, 1), :] = held
        return carry

    lax.fori_loop(0, count_x, find, 0)
    answers = []
    for step in range(1, count_y):
        peer = lax.rem(gy + step, count_y)
        answers.append(send(found.at[peer], found_x.at[gy], (gx, peer)))
    found_x[gy] = found[gy]
    for copy in answers:
        copy.wait()
    for peer in range(count_x):
        found_t[peer] = found_x[:, peer, :]
    finals = []
    for step in range(1, count_x):
        peer = lax.rem(gx + step, count_x)
        finals.append(send(found_t.at[peer], reply_out.at[gx], (peer, gy)))
    reply_out[gx] = found_t[gx]
    for copy in finals + bulk + own:
        copy.wait()
    store.wait()


def grid_steps(now, before, factor, request, disp, ids, params, count_x, count_y):
    rows = factor.shape[0]
    f32, i32 = jnp.float32, jnp.int32
    hbm = pl.BlockSpec(memory_space=pl.ANY)
    vmem = pl.BlockSpec(memory_space=pltpu.VMEM)
    halo_rows = rows + 4 * PLANE
    copies = 8 + 3 * (count_y - 1) + 2 * (count_x - 1) + 2 * (count_y - 1)
    planes = rows // PLANE
    return pl.pallas_call(
        grid_kernel,
        out_shape=(
            jax.ShapeDtypeStruct(now.shape, f32),
            jax.ShapeDtypeStruct((count_y,) + disp.shape, f32),
            jax.ShapeDtypeStruct(ids.shape, i32),
            jax.ShapeDtypeStruct(params.shape, f32),
            jax.ShapeDtypeStruct(request.shape, f32),
        ),
        in_specs=[hbm, hbm, hbm, vmem, hbm, hbm, hbm],
        out_specs=(hbm, hbm, hbm, hbm, vmem),
        scratch_shapes=[
            pltpu.VMEM((3, halo_rows, LANES), f32),
            pltpu.VMEM((3, halo_rows, LANES), f32),
            pltpu.VMEM((3, rows, LANES), f32),
            pltpu.VMEM((3, rows, LANES), f32),
            pltpu.VMEM((rows, LANES), f32),
            pltpu.VMEM((2, 2, 3, planes, 8, LANES), f32),
            pltpu.VMEM((2, 2, 3, planes, 8, LANES), f32),
            pltpu.VMEM((count_x, count_y, LANES), i32),
            pltpu.VMEM((count_y, count_x, LANES), i32),
            pltpu.VMEM((count_y, count_x, LANES), i32),
            pltpu.VMEM((count_y, count_x, LANES), i32),
            pltpu.SMEM((count_y, count_x, LANES), i32),
            pltpu.VMEM((count_y, count_x, LANES), f32),
            pltpu.VMEM((count_y, count_x, LANES), f32),
            pltpu.VMEM((count_x, count_y, LANES), f32),
            pltpu.SemaphoreType.DMA((copies,)),
            pltpu.SemaphoreType.DMA((copies,)),
            pltpu.SemaphoreType.DMA((8,)),
        ],
        compiler_params=pltpu.CompilerParams(
            vmem_limit_bytes=VMEM_LIMIT, collective_id=1, has_side_effects=True
        ),
        name="grid_steps",
    )(now, before, factor, request, disp, ids, params)


def gradient_signs(corner):
    lane = lax.broadcasted_iota(jnp.int32, (1, LANES), 1)
    signs = jnp.zeros((1, LANES), jnp.float32)
    for direction in range(3):
        value = 0.25 if (corner >> direction) & 1 else -0.25
        inside = (lane >= 3 * direction) & (lane < 3 * direction + 3)
        signs = jnp.where(inside, value, signs)
    return signs


def rows_of(values):
    count = values.shape[0]
    padded = jnp.concatenate(
        [values, jnp.zeros((SLOTS - count, LANES), jnp.float32)], axis=0
    )
    return padded.T


def box_kernel(
    layer_ref, slot_ref, ids_hbm, disp_ref, params_ref, reply_ref,
    out_ref, table, rows, layer_rows, reply_rows, counts, *rest,
):
    ids, sems, count_sem = rest[:8], rest[8], rest[9]
    owners, _, own = disp_ref.shape
    stripe = ids[0].shape[0] // owners
    span = ID_ROWS * LANES
    copies = []
    for part in range(owners):
        copies.append(
            pltpu.make_async_copy(
                ids_hbm.at[pl.ds(part * span + 8 * stripe, 1024)],
                counts.at[pl.ds(part * 1024, 1024)],
                count_sem.at[part],
            )
        )
        for corner in range(8):
            copies.append(
                pltpu.make_async_copy(
                    ids_hbm.at[pl.ds(part * span + corner * stripe, stripe)],
                    ids[corner].at[pl.ds(part * stripe, stripe)],
                    sems.at[part, corner],
                )
            )
    for copy in copies:
        copy.start()

    def build(part, carry):
        for tile in range(own // LANES):
            block = disp_ref[part, :, tile * LANES : (tile + 1) * LANES]
            lines = rows_of(jnp.concatenate([block, block, block], axis=0))
            table[pl.ds(aligned(part * own + tile * LANES), LANES), 0:SLOTS] = lines
        return carry

    lax.fori_loop(0, owners, build, 0)
    signs = [gradient_signs(corner) for corner in range(8)]
    mine = lax.axis_index("gy")

    def live_of(part):
        count = counts[part * 1024]
        whole = count // LANES
        tiles = (whole + owners - 1 - mine) // owners
        partial = jnp.where(whole % owners == mine, count % LANES, 0)
        return tiles * LANES + partial

    for copy in copies:
        copy.wait()

    for part in range(owners):

        def gather(chunk, carry, part=part):
            base = part * stripe + chunk * GATHER_UNROLL
            for step in range(GATHER_UNROLL):
                slot = base + step
                ends = [table[pl.ds(ids[corner][slot], 1), :] for corner in range(8)]
                spans = [ends[corner] - ends[7 - corner] for corner in range(4)]
                rows[pl.ds(slot, 1), :] = (spans[0] * signs[0] + spans[1] * signs[1]) + (
                    spans[2] * signs[2] + spans[3] * signs[3]
                )
            return carry

        lax.fori_loop(0, (live_of(part) + GATHER_UNROLL - 1) // GATHER_UNROLL, gather, 0)

    def layer_ends(chunk, carry):
        base = chunk * LAYER_UNROLL
        for step in range(LAYER_UNROLL):
            node = layer_ref[0, base + step]
            layer_rows[pl.ds(base + step, 1), :] = table[pl.ds(node, 1), :]
        return carry

    layers = layer_rows.shape[0]
    lax.fori_loop(0, layers // LAYER_UNROLL, layer_ends, 0)

    def clear(chunk, carry):
        zero = jnp.zeros((LANES, LANES), jnp.float32)
        table[pl.ds(aligned(chunk * LANES), LANES), :] = zero
        return carry

    lax.fori_loop(0, table.shape[0] // LANES, clear, 0)
    lane = lax.broadcasted_iota(jnp.int32, (1, LANES), 1)
    total = table
    tiles = stripe // LANES

    for part in range(owners):
        live = live_of(part)

        def element(tile, carry, part=part, live=live):
            start = aligned(part * stripe + tile * LANES)
            grads = rows[pl.ds(start, LANES), 0:SLOTS].T
            slope = [[grads[3 * j + i : 3 * j + i + 1] for j in range(3)] for i in range(3)]
            s00, s11, s22 = slope[0][0], slope[1][1], slope[2][2]
            s01 = 0.5 * (slope[0][1] + slope[1][0])
            s02 = 0.5 * (slope[0][2] + slope[2][0])
            s12 = 0.5 * (slope[1][2] + slope[2][1])
            trace = s00 + s11 + s22
            mean = trace / 3.0
            d00, d11, d22 = s00 - mean, s11 - mean, s22 - mean
            invariant = d00 * d00 + d11 * d11 + d22 * d22
            invariant = invariant + 2.0 * (s01 * s01 + s02 * s02 + s12 * s12)
            shear = params_ref[part, pl.ds(tile, 1), :]
            lame = params_ref[part, pl.ds(tiles + tile, 1), :]
            scale = params_ref[part, pl.ds(2 * tiles + tile, 1), :]
            softened = 2.0 * shear / (1.0 + invariant / scale)
            volume = lame * trace
            index = tile * LANES + lane

            def signed(value):
                return jnp.where(index < live, -value, 0.0)

            p00 = signed(volume + softened * s00)
            p11 = signed(volume + softened * s11)
            p22 = signed(volume + softened * s22)
            p01, p02, p12 = signed(softened * s01), signed(softened * s02), signed(softened * s12)
            rows[pl.ds(start, LANES), 0:SLOTS] = rows_of(
                jnp.concatenate([p00, p01, p02, p01, p11, p12, p02, p12, p22], axis=0)
            )
            return carry

        lax.fori_loop(0, (live + LANES - 1) // LANES, element, 0)

        def scatter(chunk, carry, part=part):
            base = part * stripe + chunk * SCATTER_UNROLL
            for step in range(SCATTER_UNROLL):
                line = rows[pl.ds(base + step, 1), :]
                nodes = [ids[corner][base + step] for corner in range(8)]
                terms = [line * signs[corner] for corner in range(4)]
                held = [total[pl.ds(node, 1), :] for node in nodes]
                for corner in range(8):
                    if corner < 4:
                        held[corner] = held[corner] + terms[corner]
                    else:
                        held[corner] = held[corner] - terms[7 - corner]
                for corner in range(8):
                    total[pl.ds(nodes[corner], 1), :] = held[corner]
            return carry

        lax.fori_loop(0, (live + SCATTER_UNROLL - 1) // SCATTER_UNROLL, scatter, 0)

    devices = reply_ref.shape[0]
    for position in range(LANES // SLOTS):
        values = reply_ref[...]
        if position:
            values = pltpu.roll(values, LANES - position * SLOTS, 1)
        reply_rows[position * devices : (position + 1) * devices, :] = values
    first = jnp.where(lane < 3, PENALTY, 0.0)

    def layer(chunk, carry):
        base = chunk * LAYER_UNROLL
        steps = range(LAYER_UNROLL)
        nodes = [layer_ref[0, base + step] for step in steps]
        held = [total[pl.ds(node, 1), :] for node in nodes]
        for step in steps:
            reply = reply_rows[pl.ds(slot_ref[0, base + step], 1), :]
            held[step] = held[step] + (reply - layer_rows[pl.ds(base + step, 1), :]) * first
        for step in steps:
            total[pl.ds(nodes[step], 1), :] = held[step]
        return carry

    lax.fori_loop(0, layers // LAYER_UNROLL, layer, 0)

    def fold(part, carry):
        for tile in range(own // LANES):
            start = aligned(part * own + tile * LANES)
            block = total[pl.ds(start, LANES), 0:SLOTS].T
            out_ref[part, :, tile * LANES : (tile + 1) * LANES] = (
                block[0:3] + block[3:6] + block[6:9]
            )
        return carry

    lax.fori_loop(0, owners, fold, 0)


def box_forces(layer_ids, slot_index, ids, disp, params, replies):
    owners, _, own = disp.shape
    slots = params.shape[1] * LANES // 3 * owners
    layers = layer_ids.shape[1]
    smem = pl.BlockSpec(memory_space=pltpu.SMEM)
    vmem = pl.BlockSpec(memory_space=pltpu.VMEM)
    f32, i32 = jnp.float32, jnp.int32
    return pl.pallas_call(
        box_kernel,
        out_shape=jax.ShapeDtypeStruct((owners, 3, own), f32),
        in_specs=[smem, smem, pl.BlockSpec(memory_space=pl.ANY), vmem, vmem, vmem],
        out_specs=vmem,
        scratch_shapes=[
            pltpu.VMEM((owners * own, LANES), f32),
            pltpu.VMEM((slots, LANES), f32),
            pltpu.VMEM((layers, LANES), f32),
            pltpu.VMEM((replies.shape[0] * (LANES // SLOTS), LANES), f32),
            pltpu.SMEM((owners * 1024,), i32),
        ]
        + [pltpu.SMEM((slots,), i32)] * 8
        + [pltpu.SemaphoreType.DMA((owners, 8)), pltpu.SemaphoreType.DMA((owners,))],
        compiler_params=pltpu.CompilerParams(vmem_limit_bytes=VMEM_LIMIT),
        name="box_forces",
    )(layer_ids, slot_index, ids, disp, params, replies)


def tiled_rows(field):
    lead, (rows, cols) = field.shape[:-2], field.shape[-2:]
    tiles = field.reshape(lead + (rows // 8, 8, cols // LANES, LANES))
    tiles = jnp.swapaxes(tiles, -3, -2)
    return tiles.reshape(lead[:-1] + (-1, LANES))


def untiled_rows(values, shape):
    rows, cols = shape[-2:]
    tiles = values.reshape(shape[:-2] + (rows // 8, cols // LANES, 8, LANES))
    return jnp.swapaxes(tiles, -3, -2).reshape(shape)


def on_device(
    grid_now,
    grid_before,
    wave_factor,
    layer_owner,
    layer_cell,
    box_now,
    box_before,
    node_mass,
    corner_nodes,
    live_counts,
    shear_modulus,
    lame_lambda,
    strain_scale,
    layer_nodes,
):
    count_x, count_y = lax.axis_size("gx"), lax.axis_size("gy")
    devices = count_x * count_y
    own_disp = box_now.reshape(3, -1)

    owners = layer_owner.reshape(-1)
    cell_index = layer_cell.reshape(-1)
    capacity = 2 * owners.shape[0] // devices
    rank_rows = jnp.arange(owners.shape[0])
    earlier = (rank_rows[None, :] < rank_rows[:, None]).astype(jnp.bfloat16)
    matches = owners[:, None] == jnp.arange(devices)[None, :]
    before = jnp.dot(earlier, matches.astype(jnp.bfloat16), preferred_element_type=jnp.float32)
    position = jnp.sum(jnp.where(matches, before, 0.0), axis=1).astype(jnp.int32)
    request = (
        jnp.zeros((devices * capacity,), jnp.int32)
        .at[owners * capacity + position]
        .set(cell_index, unique_indices=True)
    )
    request = jnp.pad(request.reshape(devices, capacity), ((0, 0), (0, LANES - capacity)))
    slot_index = position * devices + owners

    slots = corner_nodes.shape[2]
    tiles = slots // LANES // count_y
    ids = corner_nodes.reshape(8, tiles, count_y, LANES)
    ids = jnp.transpose(ids, (2, 0, 1, 3)).reshape(count_y, 8 * tiles, LANES)
    count_rows = jnp.broadcast_to(live_counts.reshape(1, 1, 1), (count_y, 8, LANES))
    ids = jnp.concatenate([ids, count_rows], axis=1)
    params = jnp.stack([shear_modulus, lame_lambda, strain_scale])
    params = params.reshape(3, tiles, count_y, LANES)
    params = jnp.transpose(params, (2, 0, 1, 3)).reshape(count_y, 3 * tiles, LANES)

    after, all_disp, all_ids, all_params, replies = grid_steps(
        tiled_rows(grid_now),
        tiled_rows(grid_before),
        tiled_rows(wave_factor),
        request.reshape(count_x, count_y, LANES),
        own_disp,
        ids,
        params,
        count_x,
        count_y,
    )
    node_term = box_forces(
        layer_nodes,
        slot_index.reshape(1, -1),
        all_ids.reshape(-1),
        all_disp,
        all_params,
        replies.reshape(devices, LANES),
    )
    parts = lax.all_to_all(node_term, "gy", split_axis=0, concat_axis=0, tiled=True)
    summed = jnp.sum(parts, axis=0)
    box_after = 2.0 * own_disp - box_before.reshape(3, -1) + STEP_SQUARE / node_mass * summed
    return (untiled_rows(after, grid_now.shape), box_after.reshape(box_now.shape))


def solution(mesh):
    return jax.shard_map(
        on_device,
        mesh=mesh,
        in_specs=(
            P(None, "gx", "gy", None),
            P(None, "gx", "gy", None),
            P("gx", "gy", None),
            P("gx", "gy", None),
            P("gx", "gy"),
            P(None, "gx", "gy"),
            P(None, "gx", "gy"),
            P("gx", "gy"),
            P(None, "gx", "gy"),
            P("gx", "gy"),
            P("gx", "gy"),
            P("gx", "gy"),
            P("gx", "gy"),
            P("gx", "gy"),
        ),
        out_specs=(P(None, "gx", "gy", None), P(None, "gx", "gy")),
        check_vma=False,
    )
```

```python
import jax
import jax.numpy as jnp
from jax import lax
from jax.experimental import pallas as pl
from jax.experimental.pallas import tpu as pltpu
from jax.sharding import PartitionSpec as P

PENALTY = 2.0
STEP_SQUARE = 0.25
NEAR = 16.0 / 12.0
FAR = -1.0 / 12.0
LANES = 128
SLOTS = 16
ID_ROWS = 72
PLANE = 128
VMEM_LIMIT = 58 * 2**20
GATHER_UNROLL = 16
SCATTER_UNROLL = 8
LAYER_UNROLL = 16
GROUP = 8
MESH = pl.DeviceIdType.MESH


def aligned(start, unit=LANES):
    return pl.multiple_of(start, unit)


def wave_plane(comp, index, now, before, factor, out, out_shift):
    start = aligned((index + 2) * PLANE)

    def block(offset, group, tile):
        return now[comp, pl.ds(start + offset * PLANE + (group * 4 + tile) * 8, 8), :]

    sub = lax.broadcasted_iota(jnp.int32, (8, LANES), 0)
    lane = lax.broadcasted_iota(jnp.int32, (8, LANES), 1)
    zero = jnp.zeros((8, LANES), jnp.float32)
    here = [[block(0, group, tile) for tile in range(4)] for group in range(4)]

    def neighbours(values, axis, count, position):
        sums = []
        for distance in (1, 2):
            ahead = [pltpu.roll(value, distance, axis) for value in values]
            behind = [pltpu.roll(value, count - distance, axis) for value in values]
            rows = []
            for spot in range(4):
                low = ahead[spot - 1] if spot > 0 else zero
                high = behind[spot + 1] if spot < 3 else zero
                rows.append(
                    jnp.where(position < distance, low, ahead[spot])
                    + jnp.where(position >= count - distance, high, behind[spot])
                )
            sums.append(rows)
        return sums

    along_y = [neighbours([here[g][t] for g in range(4)], 0, 8, sub) for t in range(4)]
    along_z = [neighbours(here[g], 1, LANES, lane) for g in range(4)]
    for group in range(4):
        for tile in range(4):
            row = (group * 4 + tile) * 8
            near = block(-1, group, tile) + block(1, group, tile)
            far = block(-2, group, tile) + block(2, group, tile)
            near = near + (along_y[tile][0][group] + along_z[group][0][tile])
            far = far + (along_y[tile][1][group] + along_z[group][1][tile])
            centre = here[group][tile]
            laplace = NEAR * near + FAR * far - 7.5 * centre
            place = pl.ds(aligned(index * PLANE) + row, 8)
            result = 2.0 * centre - before[comp, pl.ds(aligned(before_start(before, index)) + row, 8), :]
            out[comp, pl.ds(aligned((index + out_shift) * PLANE) + row, 8), :] = (
                result + factor[place, :] * laplace
            )


def before_start(before, index):
    shift = 2 if before.shape[1] == 20 * PLANE else 0
    return (index + shift) * PLANE


def y_edges(comp, index, source, low_out, high_out):
    start = aligned((index + 2) * PLANE)
    for tile in range(4):
        first = source[comp, pl.ds(start + tile * 8, 8), :]
        last = source[comp, pl.ds(start + 96 + tile * 8, 8), :]
        low_out[comp, index, 2 * tile : 2 * tile + 2, :] = first[0:2]
        high_out[comp, index, 2 * tile : 2 * tile + 2, :] = last[6:8]


def y_corrections(comp, index, low, high, low_weight, high_weight, factor, out, out_shift):
    sub = lax.broadcasted_iota(jnp.int32, (8, LANES), 0)
    start = aligned((index + out_shift) * PLANE)
    here = aligned(index * PLANE)
    lows = low[comp, index] * low_weight
    highs = high[comp, index] * high_weight
    for tile in range(4):
        far_row, near_row = lows[2 * tile : 2 * tile + 1], lows[2 * tile + 1 : 2 * tile + 2]
        term = jnp.where(
            sub == 0, NEAR * near_row + FAR * far_row, jnp.where(sub == 1, FAR * near_row, 0.0)
        )
        place = pl.ds(start + tile * 8, 8)
        out[comp, place, :] = out[comp, place, :] + factor[pl.ds(here + tile * 8, 8), :] * term
        near_row, far_row = highs[2 * tile : 2 * tile + 1], highs[2 * tile + 1 : 2 * tile + 2]
        term = jnp.where(
            sub == 7, NEAR * near_row + FAR * far_row, jnp.where(sub == 6, FAR * near_row, 0.0)
        )
        place = pl.ds(start + 96 + tile * 8, 8)
        out[comp, place, :] = out[comp, place, :] + factor[pl.ds(here + 96 + tile * 8, 8), :] * term


def grid_kernel(
    now_hbm, before_hbm, factor_hbm, request, disp_hbm, ids_hbm, params_hbm,
    after_hbm, disp_all, ids_all, params_all, reply_out,
    now, mid, after, before, factor, y_sent, y_got, asked_x, asked_t, asked_y, rows_vmem,
    rows_smem, found, found_x, found_t, send_sems, recv_sems, local_sems,
):
    gx, gy = lax.axis_index("gx"), lax.axis_index("gy")
    count_x, count_y = lax.axis_size("gx"), lax.axis_size("gy")
    planes = factor.shape[0] // PLANE
    edge = 2 * PLANE
    inside = pl.ds(edge, planes * PLANE)

    loads = [
        pltpu.make_async_copy(now_hbm, now.at[:, inside, :], local_sems.at[0]),
        pltpu.make_async_copy(before_hbm, before, local_sems.at[1]),
        pltpu.make_async_copy(factor_hbm, factor, local_sems.at[2]),
    ]
    for load in loads:
        load.start()

    barrier = pltpu.get_barrier_semaphore()
    for step in range(1, count_x):
        peer = lax.rem(gx + step, count_x)
        pl.semaphore_signal(barrier, inc=1, device_id=(peer, gy), device_id_type=MESH)
    for step in range(1, count_y):
        peer = lax.rem(gy + step, count_y)
        pl.semaphore_signal(barrier, inc=1, device_id=(gx, peer), device_id_type=MESH)
    pl.semaphore_wait(barrier, count_x + count_y - 2)

    used = [0]

    def send(source, target, device):
        slot = used[0]
        used[0] += 1
        copy = pltpu.make_async_remote_copy(
            src_ref=source,
            dst_ref=target,
            send_sem=send_sems.at[slot],
            recv_sem=recv_sems.at[slot],
            device_id=device,
            device_id_type=MESH,
        )
        copy.start()
        return copy

    right, left = lax.rem(gx + 1, count_x), lax.rem(gx + count_x - 1, count_x)
    upper, lower = lax.rem(gy + 1, count_y), lax.rem(gy + count_y - 1, count_y)
    top = (planes - 2) * PLANE

    def x_halo(source, shift, target):
        return [
            send(
                source.at[:, pl.ds(top + shift, edge), :],
                target.at[:, pl.ds(0, edge), :],
                (right, gy),
            ),
            send(
                source.at[:, pl.ds(shift, edge), :],
                target.at[:, pl.ds(edge + planes * PLANE, edge), :],
                (left, gy),
            ),
        ]

    def y_halo(step):
        return [
            send(y_sent.at[step, 1], y_got.at[step, 0], (gx, upper)),
            send(y_sent.at[step, 0], y_got.at[step, 1], (gx, lower)),
        ]

    def each_plane(indices, body):
        def run(comp, carry):
            for low, high in indices:
                lax.fori_loop(low, high, lambda index, c: (body(comp, index), c)[1], 0)
            return carry

        lax.fori_loop(0, 3, run, 0)

    def edges(step, source):
        each_plane(
            [(0, planes)],
            lambda comp, index: y_edges(comp, index, source, y_sent.at[step, 0], y_sent.at[step, 1]),
        )

    def clear_outside(target):
        @pl.when(gx == 0)
        def _():
            target[:, 0:edge, :] = jnp.zeros((3, edge, LANES), jnp.float32)

        @pl.when(gx == count_x - 1)
        def _():
            target[:, edge + planes * PLANE :, :] = jnp.zeros((3, edge, LANES), jnp.float32)

    low_weight = jnp.where(gy == 0, 0.0, 1.0).astype(jnp.float32)
    high_weight = jnp.where(gy == count_y - 1, 0.0, 1.0).astype(jnp.float32)

    first_x = x_halo(now_hbm, 0, now)
    asks = []
    for step in range(1, count_x):
        peer = lax.rem(gx + step, count_x)
        asks.append(send(request.at[peer], asked_x.at[gx], (peer, gy)))
    asked_x[gx] = request[gx]
    loads[0].wait()
    edges(0, now)
    first_y = y_halo(0)
    bulk = []
    for step in range(1, count_y):
        peer = lax.rem(gy + step, count_y)
        bulk.append(send(disp_hbm, disp_all.at[gy], (gx, peer)))
        bulk.append(send(ids_hbm.at[step], ids_all.at[gy], (gx, peer)))
        bulk.append(send(params_hbm.at[step], params_all.at[gy], (gx, peer)))
    own = [
        pltpu.make_async_copy(disp_hbm, disp_all.at[gy], local_sems.at[3]),
        pltpu.make_async_copy(ids_hbm.at[0], ids_all.at[gy], local_sems.at[4]),
        pltpu.make_async_copy(params_hbm.at[0], params_all.at[gy], local_sems.at[5]),
    ]
    for copy in own:
        copy.start()
    loads[1].wait()
    loads[2].wait()

    def step_of(source, previous, target, shift):
        return lambda comp, index: wave_plane(comp, index, source, previous, factor, target, shift)

    def fix(step, target, shift):
        each_plane(
            [(0, planes)],
            lambda comp, index: y_corrections(
                comp, index, y_got.at[step, 0], y_got.at[step, 1], low_weight, high_weight,
                factor, target, shift,
            ),
        )

    inner, outer = [(2, planes - 2)], [(0, 2), (planes - 2, planes)]
    first = step_of(now, before, mid, 2)
    each_plane(inner, first)
    for copy in asks:
        copy.wait()
    for peer in range(count_y):
        asked_t[peer] = asked_x[:, peer, :]
    passes = []
    for step in range(1, count_y):
        peer = lax.rem(gy + step, count_y)
        passes.append(send(asked_t.at[peer], asked_y.at[gy], (gx, peer)))
    asked_y[gy] = asked_t[gy]
    for copy in first_x:
        copy.wait()
    clear_outside(now)
    each_plane(outer, first)
    for copy in first_y:
        copy.wait()
    fix(0, mid, 2)

    second_x = x_halo(mid, edge, mid)
    edges(1, mid)
    second_y = y_halo(1)
    second = step_of(mid, now, after, 0)
    each_plane(inner, second)
    for copy in passes:
        copy.wait()
    cell = asked_y[...]
    plane, row, col = cell >> 14, (cell >> 9) & 31, cell & 511
    rows_vmem[...] = (((plane * 4 + (row >> 3)) * 4 + (col >> 7)) * 8 + (row & 7)) * LANES + (
        col & (LANES - 1)
    )
    to_smem = pltpu.make_async_copy(rows_vmem, rows_smem, local_sems.at[6])
    to_smem.start()
    for copy in second_x:
        copy.wait()
    clear_outside(mid)
    each_plane(outer, second)
    for copy in second_y:
        copy.wait()
    fix(1, after, 0)
    store = pltpu.make_async_copy(after, after_hbm, local_sems.at[7])
    store.start()
    to_smem.wait()

    lane = lax.broadcasted_iota(jnp.int32, (1, LANES), 1)
    capacity = LANES // SLOTS

    def find(source, carry):
        for part in range(count_y):
            held = jnp.zeros((1, LANES), jnp.float32)
            for position in range(capacity):
                place = rows_smem[part, source, position]
                line = place >> 7
                for comp in range(3):
                    spot = position * SLOTS + comp
                    values = after[comp, pl.ds(line, 1), :]
                    shift = (spot - place) & (LANES - 1)
                    held = jnp.where(lane == spot, pltpu.roll(values, shift, 1), held)
            found[part, pl.ds(source, 1), :] = held
        return carry

    lax.fori_loop(0, count_x, find, 0)
    answers = []
    for step in range(1, count_y):
        peer = lax.rem(gy + step, count_y)
        answers.append(send(found.at[peer], found_x.at[gy], (gx, peer)))
    found_x[gy] = found[gy]
    for copy in answers:
        copy.wait()
    for peer in range(count_x):
        found_t[peer] = found_x[:, peer, :]
    finals = []
    for step in range(1, count_x):
        peer = lax.rem(gx + step, count_x)
        finals.append(send(found_t.at[peer], reply_out.at[gx], (peer, gy)))
    reply_out[gx] = found_t[gx]
    for copy in finals + bulk + own:
        copy.wait()
    store.wait()


def grid_steps(now, before, factor, request, disp, ids, params, count_x, count_y):
    rows = factor.shape[0]
    f32, i32 = jnp.float32, jnp.int32
    hbm = pl.BlockSpec(memory_space=pl.ANY)
    vmem = pl.BlockSpec(memory_space=pltpu.VMEM)
    halo_rows = rows + 4 * PLANE
    copies = 8 + 3 * (count_y - 1) + 2 * (count_x - 1) + 2 * (count_y - 1)
    planes = rows // PLANE
    return pl.pallas_call(
        grid_kernel,
        out_shape=(
            jax.ShapeDtypeStruct(now.shape, f32),
            jax.ShapeDtypeStruct((count_y,) + disp.shape, f32),
            jax.ShapeDtypeStruct(ids.shape, i32),
            jax.ShapeDtypeStruct(params.shape, f32),
            jax.ShapeDtypeStruct(request.shape, f32),
        ),
        in_specs=[hbm, hbm, hbm, vmem, hbm, hbm, hbm],
        out_specs=(hbm, hbm, hbm, hbm, vmem),
        scratch_shapes=[
            pltpu.VMEM((3, halo_rows, LANES), f32),
            pltpu.VMEM((3, halo_rows, LANES), f32),
            pltpu.VMEM((3, rows, LANES), f32),
            pltpu.VMEM((3, rows, LANES), f32),
            pltpu.VMEM((rows, LANES), f32),
            pltpu.VMEM((2, 2, 3, planes, 8, LANES), f32),
            pltpu.VMEM((2, 2, 3, planes, 8, LANES), f32),
            pltpu.VMEM((count_x, count_y, LANES), i32),
            pltpu.VMEM((count_y, count_x, LANES), i32),
            pltpu.VMEM((count_y, count_x, LANES), i32),
            pltpu.VMEM((count_y, count_x, LANES), i32),
            pltpu.SMEM((count_y, count_x, LANES), i32),
            pltpu.VMEM((count_y, count_x, LANES), f32),
            pltpu.VMEM((count_y, count_x, LANES), f32),
            pltpu.VMEM((count_x, count_y, LANES), f32),
            pltpu.SemaphoreType.DMA((copies,)),
            pltpu.SemaphoreType.DMA((copies,)),
            pltpu.SemaphoreType.DMA((8,)),
        ],
        compiler_params=pltpu.CompilerParams(
            vmem_limit_bytes=VMEM_LIMIT, collective_id=1, has_side_effects=True
        ),
        name="grid_steps",
    )(now, before, factor, request, disp, ids, params)


def gradient_signs(corner):
    lane = lax.broadcasted_iota(jnp.int32, (1, LANES), 1)
    signs = jnp.zeros((1, LANES), jnp.float32)
    for direction in range(3):
        value = 0.25 if (corner >> direction) & 1 else -0.25
        inside = (lane >= 3 * direction) & (lane < 3 * direction + 3)
        signs = jnp.where(inside, value, signs)
    return signs


def rows_of(values):
    count = values.shape[0]
    padded = jnp.concatenate(
        [values, jnp.zeros((SLOTS - count, LANES), jnp.float32)], axis=0
    )
    return padded.T


def box_kernel(
    layer_ref, slot_ref, ids_hbm, disp_ref, params_ref, reply_ref, field_in,
    out_ref, field_out, table, rows, layer_rows, reply_rows, field, counts, *rest,
):
    ids, sems, count_sem, field_sem = rest[:8], rest[8], rest[9], rest[10]
    owners, _, own = disp_ref.shape
    stripe = ids[0].shape[0] // owners
    span = ID_ROWS * LANES
    copies = []
    for part in range(owners):
        copies.append(
            pltpu.make_async_copy(
                ids_hbm.at[pl.ds(part * span + 8 * stripe, 1024)],
                counts.at[pl.ds(part * 1024, 1024)],
                count_sem.at[part],
            )
        )
        for corner in range(8):
            copies.append(
                pltpu.make_async_copy(
                    ids_hbm.at[pl.ds(part * span + corner * stripe, stripe)],
                    ids[corner].at[pl.ds(part * stripe, stripe)],
                    sems.at[part, corner],
                )
            )
    for copy in copies:
        copy.start()
    field_load = pltpu.make_async_copy(field_in, field, field_sem.at[0])
    field_load.start()

    def build(part, carry):
        for tile in range(own // LANES):
            block = disp_ref[part, :, tile * LANES : (tile + 1) * LANES]
            lines = rows_of(jnp.concatenate([block, block, block], axis=0))
            table[pl.ds(aligned(part * own + tile * LANES), LANES), 0:SLOTS] = lines
        return carry

    lax.fori_loop(0, owners, build, 0)
    field_load.wait()
    field_store = pltpu.make_async_copy(field, field_out, field_sem.at[1])
    field_store.start()
    signs = [gradient_signs(corner) for corner in range(8)]
    mine = lax.axis_index("gy")

    def live_of(part):
        count = counts[part * 1024]
        whole = count // LANES
        turn = lax.rem(mine - part + owners, owners)
        tiles = (whole + owners - 1 - turn) // owners
        partial = jnp.where(whole % owners == turn, count % LANES, 0)
        return tiles * LANES + partial


    for part in range(owners):
        for copy in copies[9 * part : 9 * part + 9]:
            copy.wait()

        def gather(chunk, carry, part=part):
            base = part * stripe + chunk * GATHER_UNROLL
            for step in range(GATHER_UNROLL):
                slot = base + step
                ends = [table[pl.ds(ids[corner][slot], 1), :] for corner in range(8)]
                spans = [ends[corner] - ends[7 - corner] for corner in range(4)]
                rows[pl.ds(slot, 1), :] = (spans[0] * signs[0] + spans[1] * signs[1]) + (
                    spans[2] * signs[2] + spans[3] * signs[3]
                )
            return carry

        lax.fori_loop(0, (live_of(part) + GATHER_UNROLL - 1) // GATHER_UNROLL, gather, 0)

    def layer_ends(chunk, carry):
        base = chunk * LAYER_UNROLL
        for step in range(LAYER_UNROLL):
            node = layer_ref[0, base + step]
            layer_rows[pl.ds(base + step, 1), :] = table[pl.ds(node, 1), :]
        return carry

    layers = layer_rows.shape[0]
    lax.fori_loop(0, layers // LAYER_UNROLL, layer_ends, 0)

    def clear(chunk, carry):
        zero = jnp.zeros((LANES, LANES), jnp.float32)
        table[pl.ds(aligned(chunk * LANES), LANES), :] = zero
        return carry

    lax.fori_loop(0, table.shape[0] // LANES, clear, 0)
    lane = lax.broadcasted_iota(jnp.int32, (1, LANES), 1)
    total = table
    tiles = stripe // LANES

    for part in range(owners):
        live = live_of(part)

        def element(tile, carry, part=part, live=live):
            start = aligned(part * stripe + tile * LANES)
            grads = rows[pl.ds(start, LANES), 0:SLOTS].T
            slope = [[grads[3 * j + i : 3 * j + i + 1] for j in range(3)] for i in range(3)]
            s00, s11, s22 = slope[0][0], slope[1][1], slope[2][2]
            s01 = 0.5 * (slope[0][1] + slope[1][0])
            s02 = 0.5 * (slope[0][2] + slope[2][0])
            s12 = 0.5 * (slope[1][2] + slope[2][1])
            trace = s00 + s11 + s22
            mean = trace / 3.0
            d00, d11, d22 = s00 - mean, s11 - mean, s22 - mean
            invariant = d00 * d00 + d11 * d11 + d22 * d22
            invariant = invariant + 2.0 * (s01 * s01 + s02 * s02 + s12 * s12)
            shear = params_ref[part, pl.ds(tile, 1), :]
            lame = params_ref[part, pl.ds(tiles + tile, 1), :]
            scale = params_ref[part, pl.ds(2 * tiles + tile, 1), :]
            softened = 2.0 * shear / (1.0 + invariant / scale)
            volume = lame * trace
            index = tile * LANES + lane

            def signed(value):
                return jnp.where(index < live, -0.25 * value, 0.0)

            p00 = signed(volume + softened * s00)
            p11 = signed(volume + softened * s11)
            p22 = signed(volume + softened * s22)
            p01, p02, p12 = signed(softened * s01), signed(softened * s02), signed(softened * s12)
            pad = jnp.zeros((GROUP - 3, LANES), jnp.float32)
            sides = [
                jnp.concatenate(column + [pad], axis=0)
                for column in ([p00, p01, p02], [p01, p11, p12], [p02, p12, p22])
            ]
            ends = []
            for corner in range(4):
                term = sides[0] if corner & 1 else -sides[0]
                term = term + sides[1] if corner & 2 else term - sides[1]
                ends.append(term - sides[2])
            ends += [-ends[7 - corner] for corner in range(4, 8)]
            rows[pl.ds(start, LANES), 0 : 8 * GROUP] = jnp.concatenate(ends, axis=0).T
            return carry

        lax.fori_loop(0, (live + LANES - 1) // LANES, element, 0)

        def scatter(chunk, carry, part=part):
            base = part * stripe + chunk * SCATTER_UNROLL
            for step in range(SCATTER_UNROLL):
                line = rows[pl.ds(base + step, 1), :]
                for corner in range(8):
                    own_lanes = slice(corner * GROUP, (corner + 1) * GROUP)
                    total[pl.ds(ids[corner][base + step], 1), own_lanes] = line[:, own_lanes]
            return carry

        lax.fori_loop(0, (live + SCATTER_UNROLL - 1) // SCATTER_UNROLL, scatter, 0)

    devices = reply_ref.shape[0]
    for position in range(LANES // SLOTS):
        values = reply_ref[...]
        if position:
            values = pltpu.roll(values, LANES - position * SLOTS, 1)
        reply_rows[position * devices : (position + 1) * devices, :] = values
    inside = lane < 3

    def layer(chunk, carry):
        base = chunk * LAYER_UNROLL
        steps = range(LAYER_UNROLL)
        nodes = [layer_ref[0, base + step] for step in steps]
        held = [total[pl.ds(node, 1), :] for node in nodes]
        for step in steps:
            reply = reply_rows[pl.ds(slot_ref[0, base + step], 1), :]
            gap = reply - layer_rows[pl.ds(base + step, 1), :]
            held[step] = held[step] + jnp.where(inside, PENALTY * gap, 0.0)
        for step in steps:
            total[pl.ds(nodes[step], 1), :] = held[step]
        return carry

    lax.fori_loop(0, layers // LAYER_UNROLL, layer, 0)

    def fold(part, carry):
        for tile in range(own // LANES):
            start = aligned(part * own + tile * LANES)
            block = total[pl.ds(start, LANES), 0 : 8 * GROUP].T
            terms = [block[corner * GROUP : corner * GROUP + GROUP] for corner in range(8)]
            while len(terms) > 1:
                terms = [a + b for a, b in zip(terms[0::2], terms[1::2])]
            out_ref[part, :, tile * LANES : (tile + 1) * LANES] = terms[0][0:3]
        return carry

    lax.fori_loop(0, owners, fold, 0)
    field_store.wait()


def box_forces(layer_ids, slot_index, ids, disp, params, replies, field):
    owners, _, own = disp.shape
    slots = params.shape[1] * LANES // 3 * owners
    layers = layer_ids.shape[1]
    smem = pl.BlockSpec(memory_space=pltpu.SMEM)
    vmem = pl.BlockSpec(memory_space=pltpu.VMEM)
    hbm = pl.BlockSpec(memory_space=pl.ANY)
    f32, i32 = jnp.float32, jnp.int32
    return pl.pallas_call(
        box_kernel,
        out_shape=(
            jax.ShapeDtypeStruct((owners, 3, own), f32),
            jax.ShapeDtypeStruct(field.shape, f32),
        ),
        in_specs=[smem, smem, hbm, vmem, vmem, vmem, hbm],
        out_specs=(vmem, hbm),
        scratch_shapes=[
            pltpu.VMEM((owners * own, LANES), f32),
            pltpu.VMEM((slots, LANES), f32),
            pltpu.VMEM((layers, LANES), f32),
            pltpu.VMEM((replies.shape[0] * (LANES // SLOTS), LANES), f32),
            pltpu.VMEM(field.shape, f32),
            pltpu.SMEM((owners * 1024,), i32),
        ]
        + [pltpu.SMEM((slots,), i32)] * 8
        + [
            pltpu.SemaphoreType.DMA((owners, 8)),
            pltpu.SemaphoreType.DMA((owners,)),
            pltpu.SemaphoreType.DMA((2,)),
        ],
        compiler_params=pltpu.CompilerParams(vmem_limit_bytes=VMEM_LIMIT),
        name="box_forces",
    )(layer_ids, slot_index, ids, disp, params, replies, field)


def tiled_rows(field):
    lead, (rows, cols) = field.shape[:-2], field.shape[-2:]
    tiles = field.reshape(lead + (rows // 8, 8, cols // LANES, LANES))
    tiles = jnp.swapaxes(tiles, -3, -2)
    return tiles.reshape(lead[:-1] + (-1, LANES))


def untiled_rows(values, shape):
    rows, cols = shape[-2:]
    tiles = values.reshape(shape[:-2] + (rows // 8, cols // LANES, 8, LANES))
    return jnp.swapaxes(tiles, -3, -2).reshape(shape)


def on_device(
    grid_now,
    grid_before,
    wave_factor,
    layer_owner,
    layer_cell,
    box_now,
    box_before,
    node_mass,
    corner_nodes,
    live_counts,
    shear_modulus,
    lame_lambda,
    strain_scale,
    layer_nodes,
):
    count_x, count_y = lax.axis_size("gx"), lax.axis_size("gy")
    devices = count_x * count_y
    own_disp = box_now.reshape(3, -1)

    owners = layer_owner.reshape(-1)
    cell_index = layer_cell.reshape(-1)
    capacity = 2 * owners.shape[0] // devices
    rank_rows = jnp.arange(owners.shape[0])
    earlier = (rank_rows[None, :] < rank_rows[:, None]).astype(jnp.bfloat16)
    matches = owners[:, None] == jnp.arange(devices)[None, :]
    before = jnp.dot(earlier, matches.astype(jnp.bfloat16), preferred_element_type=jnp.float32)
    position = jnp.sum(jnp.where(matches, before, 0.0), axis=1).astype(jnp.int32)
    request = (
        jnp.zeros((devices * capacity,), jnp.int32)
        .at[owners * capacity + position]
        .set(cell_index, unique_indices=True)
    )
    request = jnp.pad(request.reshape(devices, capacity), ((0, 0), (0, LANES - capacity)))
    slot_index = position * devices + owners

    slots = corner_nodes.shape[2]
    tiles = slots // LANES // count_y
    ids = corner_nodes.reshape(8, tiles, count_y, LANES)
    ids = jnp.transpose(ids, (2, 0, 1, 3)).reshape(count_y, 8 * tiles, LANES)
    count_rows = jnp.broadcast_to(live_counts.reshape(1, 1, 1), (count_y, 8, LANES))
    ids = jnp.concatenate([ids, count_rows], axis=1)
    params = jnp.stack([shear_modulus, lame_lambda, strain_scale])
    params = params.reshape(3, tiles, count_y, LANES)
    params = jnp.transpose(params, (2, 0, 1, 3)).reshape(count_y, 3 * tiles, LANES)

    after, all_disp, all_ids, all_params, replies = grid_steps(
        tiled_rows(grid_now),
        tiled_rows(grid_before),
        tiled_rows(wave_factor),
        request.reshape(count_x, count_y, LANES),
        own_disp,
        ids,
        params,
        count_x,
        count_y,
    )
    node_term, after = box_forces(
        layer_nodes,
        slot_index.reshape(1, -1),
        all_ids.reshape(-1),
        all_disp,
        all_params,
        replies.reshape(devices, LANES),
        after,
    )
    parts = lax.all_to_all(node_term, "gy", split_axis=0, concat_axis=0, tiled=True)
    summed = jnp.sum(parts, axis=0)
    box_after = 2.0 * own_disp - box_before.reshape(3, -1) + STEP_SQUARE / node_mass * summed
    return (untiled_rows(after, grid_now.shape), box_after.reshape(box_now.shape))


def solution(mesh):
    return jax.shard_map(
        on_device,
        mesh=mesh,
        in_specs=(
            P(None, "gx", "gy", None),
            P(None, "gx", "gy", None),
            P("gx", "gy", None),
            P("gx", "gy", None),
            P("gx", "gy"),
            P(None, "gx", "gy"),
            P(None, "gx", "gy"),
            P("gx", "gy"),
            P(None, "gx", "gy"),
            P("gx", "gy"),
            P("gx", "gy"),
            P("gx", "gy"),
            P("gx", "gy"),
            P("gx", "gy"),
        ),
        out_specs=(P(None, "gx", "gy", None), P(None, "gx", "gy")),
        check_vma=False,
    )
```

```python
import jax
import jax.numpy as jnp
from jax import lax
from jax.experimental import pallas as pl
from jax.experimental.pallas import tpu as pltpu
from jax.sharding import PartitionSpec as P

PENALTY = 2.0
STEP_SQUARE = 0.25
NEAR = 16.0 / 12.0
FAR = -1.0 / 12.0
LANES = 128
SLOTS = 16
ID_ROWS = 72
PLANE = 128
VMEM_LIMIT = 58 * 2**20
GATHER_UNROLL = 16
SCATTER_UNROLL = 8
LAYER_UNROLL = 16
GROUP = 8
MESH = pl.DeviceIdType.MESH


def aligned(start, unit=LANES):
    return pl.multiple_of(start, unit)


def rank_kernel(owner_ref, cell_ref, request_out, slot_out):
    devices, layers = request_out.shape[0], owner_ref.shape[1]
    row = lax.broadcasted_iota(jnp.int32, (devices, layers), 0)
    owner, cell = owner_ref[...], cell_ref[...]
    found = row == owner
    matches = jnp.where(found, 1.0, 0.0).astype(jnp.bfloat16)
    first = lax.broadcasted_iota(jnp.int32, (layers, layers), 0)
    second = lax.broadcasted_iota(jnp.int32, (layers, layers), 1)
    earlier = jnp.where(first < second, 1.0, 0.0).astype(jnp.bfloat16)
    before = jnp.dot(matches, earlier, preferred_element_type=jnp.float32)
    position = jnp.sum(jnp.where(found, before, 0.0), axis=0, keepdims=True).astype(jnp.int32)
    placed = row == position
    request = jnp.zeros((devices, devices), jnp.int32)
    for shift in (0, 6, 12):
        digit = ((cell >> shift) & 63).astype(jnp.float32)
        digits = jnp.where(placed, digit, 0.0).astype(jnp.bfloat16)
        part = lax.dot_general(
            matches, digits, (((1,), (1,)), ((), ())), preferred_element_type=jnp.float32
        )
        request = request + (part.astype(jnp.int32) << shift)
    request_out[...] = request
    slot_out[...] = position * devices + owner


def rank_requests(owners, cells, devices):
    vmem = pl.BlockSpec(memory_space=pltpu.VMEM)
    return pl.pallas_call(
        rank_kernel,
        out_shape=(
            jax.ShapeDtypeStruct((devices, LANES), jnp.int32),
            jax.ShapeDtypeStruct(owners.shape, jnp.int32),
        ),
        in_specs=[vmem, vmem],
        out_specs=(vmem, vmem),
        name="rank_requests",
    )(owners, cells)


def wave_plane(comp, index, now, before, factor, out, out_shift):
    start = aligned((index + 2) * PLANE)

    def block(offset, group, tile):
        return now[comp, pl.ds(start + offset * PLANE + (group * 4 + tile) * 8, 8), :]

    sub = lax.broadcasted_iota(jnp.int32, (8, LANES), 0)
    lane = lax.broadcasted_iota(jnp.int32, (8, LANES), 1)
    zero = jnp.zeros((8, LANES), jnp.float32)
    here = [[block(0, group, tile) for tile in range(4)] for group in range(4)]

    def neighbours(values, axis, count, position):
        sums = []
        for distance in (1, 2):
            ahead = [pltpu.roll(value, distance, axis) for value in values]
            behind = [pltpu.roll(value, count - distance, axis) for value in values]
            rows = []
            for spot in range(4):
                low = ahead[spot - 1] if spot > 0 else zero
                high = behind[spot + 1] if spot < 3 else zero
                rows.append(
                    jnp.where(position < distance, low, ahead[spot])
                    + jnp.where(position >= count - distance, high, behind[spot])
                )
            sums.append(rows)
        return sums

    along_y = [neighbours([here[g][t] for g in range(4)], 0, 8, sub) for t in range(4)]
    along_z = [neighbours(here[g], 1, LANES, lane) for g in range(4)]
    for group in range(4):
        for tile in range(4):
            row = (group * 4 + tile) * 8
            near = block(-1, group, tile) + block(1, group, tile)
            far = block(-2, group, tile) + block(2, group, tile)
            near = near + (along_y[tile][0][group] + along_z[group][0][tile])
            far = far + (along_y[tile][1][group] + along_z[group][1][tile])
            centre = here[group][tile]
            laplace = NEAR * near + FAR * far - 7.5 * centre
            place = pl.ds(aligned(index * PLANE) + row, 8)
            result = 2.0 * centre - before[comp, pl.ds(aligned(before_start(before, index)) + row, 8), :]
            out[comp, pl.ds(aligned((index + out_shift) * PLANE) + row, 8), :] = (
                result + factor[place, :] * laplace
            )


def before_start(before, index):
    shift = 2 if before.shape[1] == 20 * PLANE else 0
    return (index + shift) * PLANE


def y_edges(comp, index, source, low_out, high_out):
    start = aligned((index + 2) * PLANE)
    for tile in range(4):
        first = source[comp, pl.ds(start + tile * 8, 8), :]
        last = source[comp, pl.ds(start + 96 + tile * 8, 8), :]
        low_out[comp, index, 2 * tile : 2 * tile + 2, :] = first[0:2]
        high_out[comp, index, 2 * tile : 2 * tile + 2, :] = last[6:8]


def y_corrections(comp, index, low, high, low_weight, high_weight, factor, out, out_shift):
    sub = lax.broadcasted_iota(jnp.int32, (8, LANES), 0)
    start = aligned((index + out_shift) * PLANE)
    here = aligned(index * PLANE)
    lows = low[comp, index] * low_weight
    highs = high[comp, index] * high_weight
    for tile in range(4):
        far_row, near_row = lows[2 * tile : 2 * tile + 1], lows[2 * tile + 1 : 2 * tile + 2]
        term = jnp.where(
            sub == 0, NEAR * near_row + FAR * far_row, jnp.where(sub == 1, FAR * near_row, 0.0)
        )
        place = pl.ds(start + tile * 8, 8)
        out[comp, place, :] = out[comp, place, :] + factor[pl.ds(here + tile * 8, 8), :] * term
        near_row, far_row = highs[2 * tile : 2 * tile + 1], highs[2 * tile + 1 : 2 * tile + 2]
        term = jnp.where(
            sub == 7, NEAR * near_row + FAR * far_row, jnp.where(sub == 6, FAR * near_row, 0.0)
        )
        place = pl.ds(start + 96 + tile * 8, 8)
        out[comp, place, :] = out[comp, place, :] + factor[pl.ds(here + 96 + tile * 8, 8), :] * term


def grid_kernel(
    now_hbm, before_hbm, factor_hbm, request, disp_raw, ids_raw, shear_raw, lame_raw, scale_raw, live,
    after_hbm, disp_all, ids_all, params_all, reply_out,
    now, mid, after, before, factor, y_sent, y_got, asked_x, asked_t, asked_y, rows_vmem,
    rows_smem, found, found_x, found_t, disp_own, ids_own, params_own, send_sems, recv_sems, local_sems,
):
    gx, gy = lax.axis_index("gx"), lax.axis_index("gy")
    count_x, count_y = lax.axis_size("gx"), lax.axis_size("gy")
    planes = factor.shape[0] // PLANE
    edge = 2 * PLANE
    inside = pl.ds(edge, planes * PLANE)

    loads = [
        pltpu.make_async_copy(now_hbm, now.at[:, inside, :], local_sems.at[0]),
        pltpu.make_async_copy(before_hbm, before, local_sems.at[1]),
        pltpu.make_async_copy(factor_hbm, factor, local_sems.at[2]),
    ]
    for load in loads:
        load.start()

    barrier = pltpu.get_barrier_semaphore()
    for step in range(1, count_x):
        peer = lax.rem(gx + step, count_x)
        pl.semaphore_signal(barrier, inc=1, device_id=(peer, gy), device_id_type=MESH)
    for step in range(1, count_y):
        peer = lax.rem(gy + step, count_y)
        pl.semaphore_signal(barrier, inc=1, device_id=(gx, peer), device_id_type=MESH)
    pl.semaphore_wait(barrier, count_x + count_y - 2)

    used = [0]

    def send(source, target, device):
        slot = used[0]
        used[0] += 1
        copy = pltpu.make_async_remote_copy(
            src_ref=source,
            dst_ref=target,
            send_sem=send_sems.at[slot],
            recv_sem=recv_sems.at[slot],
            device_id=device,
            device_id_type=MESH,
        )
        copy.start()
        return copy

    right, left = lax.rem(gx + 1, count_x), lax.rem(gx + count_x - 1, count_x)
    upper, lower = lax.rem(gy + 1, count_y), lax.rem(gy + count_y - 1, count_y)
    top = (planes - 2) * PLANE

    def x_halo(source, shift, target):
        return [
            send(
                source.at[:, pl.ds(top + shift, edge), :],
                target.at[:, pl.ds(0, edge), :],
                (right, gy),
            ),
            send(
                source.at[:, pl.ds(shift, edge), :],
                target.at[:, pl.ds(edge + planes * PLANE, edge), :],
                (left, gy),
            ),
        ]

    def y_halo(step):
        return [
            send(y_sent.at[step, 1], y_got.at[step, 0], (gx, upper)),
            send(y_sent.at[step, 0], y_got.at[step, 1], (gx, lower)),
        ]

    def each_plane(indices, body):
        def run(comp, carry):
            for low, high in indices:
                lax.fori_loop(low, high, lambda index, c: (body(comp, index), c)[1], 0)
            return carry

        lax.fori_loop(0, 3, run, 0)

    def edges(step, source):
        each_plane(
            [(0, planes)],
            lambda comp, index: y_edges(comp, index, source, y_sent.at[step, 0], y_sent.at[step, 1]),
        )

    def clear_outside(target):
        @pl.when(gx == 0)
        def _():
            target[:, 0:edge, :] = jnp.zeros((3, edge, LANES), jnp.float32)

        @pl.when(gx == count_x - 1)
        def _():
            target[:, edge + planes * PLANE :, :] = jnp.zeros((3, edge, LANES), jnp.float32)

    low_weight = jnp.where(gy == 0, 0.0, 1.0).astype(jnp.float32)
    high_weight = jnp.where(gy == count_y - 1, 0.0, 1.0).astype(jnp.float32)

    first_x = x_halo(now_hbm, 0, now)
    asks = []
    for step in range(1, count_x):
        peer = lax.rem(gx + step, count_x)
        asks.append(send(request.at[peer], asked_x.at[gx], (peer, gy)))
    asked_x[gx] = request[gx]
    loads[0].wait()
    edges(0, now)
    first_y = y_halo(0)
    for comp in range(3):
        for tile in range(disp_raw.shape[1]):
            disp_own[comp : comp + 1, tile * LANES : (tile + 1) * LANES] = disp_raw[comp, tile]
    stripes = ids_raw.shape[1] // count_y
    for turn in range(count_y):
        every = pl.ds(turn, stripes, stride=count_y)
        for corner in range(8):
            here = slice(corner * stripes, (corner + 1) * stripes)
            ids_own[turn, here, :] = ids_raw[corner, every, :]
        ids_own[turn, 8 * stripes :, :] = jnp.full((8, LANES), live[0, 0], jnp.int32)
        for index, raw in enumerate((shear_raw, lame_raw, scale_raw)):
            here = slice(index * stripes, (index + 1) * stripes)
            params_own[turn, here, :] = raw[every, :]
    bulk = []
    for step in range(1, count_y):
        peer = lax.rem(gy + step, count_y)
        bulk.append(send(disp_own, disp_all.at[gy], (gx, peer)))
        bulk.append(send(ids_own.at[step], ids_all.at[gy], (gx, peer)))
        bulk.append(send(params_own.at[step], params_all.at[gy], (gx, peer)))
    own = [
        pltpu.make_async_copy(disp_own, disp_all.at[gy], local_sems.at[3]),
        pltpu.make_async_copy(ids_own.at[0], ids_all.at[gy], local_sems.at[4]),
        pltpu.make_async_copy(params_own.at[0], params_all.at[gy], local_sems.at[5]),
    ]
    for copy in own:
        copy.start()
    loads[1].wait()
    loads[2].wait()

    def step_of(source, previous, target, shift):
        return lambda comp, index: wave_plane(comp, index, source, previous, factor, target, shift)

    def fix(step, target, shift):
        each_plane(
            [(0, planes)],
            lambda comp, index: y_corrections(
                comp, index, y_got.at[step, 0], y_got.at[step, 1], low_weight, high_weight,
                factor, target, shift,
            ),
        )

    inner, outer = [(2, planes - 2)], [(0, 2), (planes - 2, planes)]
    first = step_of(now, before, mid, 2)
    each_plane(inner, first)
    for copy in asks:
        copy.wait()
    for peer in range(count_y):
        asked_t[peer] = asked_x[:, peer, :]
    passes = []
    for step in range(1, count_y):
        peer = lax.rem(gy + step, count_y)
        passes.append(send(asked_t.at[peer], asked_y.at[gy], (gx, peer)))
    asked_y[gy] = asked_t[gy]
    for copy in first_x:
        copy.wait()
    clear_outside(now)
    each_plane(outer, first)
    for copy in first_y:
        copy.wait()
    fix(0, mid, 2)

    second_x = x_halo(mid, edge, mid)
    edges(1, mid)
    second_y = y_halo(1)
    second = step_of(mid, now, after, 0)
    each_plane(inner, second)
    for copy in passes:
        copy.wait()
    cell = asked_y[...]
    plane, row, col = cell >> 14, (cell >> 9) & 31, cell & 511
    rows_vmem[...] = (((plane * 4 + (row >> 3)) * 4 + (col >> 7)) * 8 + (row & 7)) * LANES + (
        col & (LANES - 1)
    )
    to_smem = pltpu.make_async_copy(rows_vmem, rows_smem, local_sems.at[6])
    to_smem.start()
    for copy in second_x:
        copy.wait()
    clear_outside(mid)
    each_plane(outer, second)
    for copy in second_y:
        copy.wait()
    fix(1, after, 0)
    store = pltpu.make_async_copy(after, after_hbm, local_sems.at[7])
    store.start()
    to_smem.wait()

    lane = lax.broadcasted_iota(jnp.int32, (1, LANES), 1)
    capacity = LANES // SLOTS

    def find(source, carry):
        for part in range(count_y):
            held = jnp.zeros((1, LANES), jnp.float32)
            for position in range(capacity):
                place = rows_smem[part, source, position]
                line = place >> 7
                for comp in range(3):
                    spot = position * SLOTS + comp
                    values = after[comp, pl.ds(line, 1), :]
                    shift = (spot - place) & (LANES - 1)
                    held = jnp.where(lane == spot, pltpu.roll(values, shift, 1), held)
            found[part, pl.ds(source, 1), :] = held
        return carry

    lax.fori_loop(0, count_x, find, 0)
    answers = []
    for step in range(1, count_y):
        peer = lax.rem(gy + step, count_y)
        answers.append(send(found.at[peer], found_x.at[gy], (gx, peer)))
    found_x[gy] = found[gy]
    for copy in answers:
        copy.wait()
    for peer in range(count_x):
        found_t[peer] = found_x[:, peer, :]
    finals = []
    for step in range(1, count_x):
        peer = lax.rem(gx + step, count_x)
        finals.append(send(found_t.at[peer], reply_out.at[gx], (peer, gy)))
    reply_out[gx] = found_t[gx]
    for copy in finals + bulk + own:
        copy.wait()
    store.wait()


def grid_steps(now, before, factor, request, disp, ids, params, live, count_x, count_y):
    rows = factor.shape[0]
    f32, i32 = jnp.float32, jnp.int32
    hbm = pl.BlockSpec(memory_space=pl.ANY)
    vmem = pl.BlockSpec(memory_space=pltpu.VMEM)
    halo_rows = rows + 4 * PLANE
    copies = 8 + 3 * (count_y - 1) + 2 * (count_x - 1) + 2 * (count_y - 1)
    planes = rows // PLANE
    stripes = ids.shape[1] // count_y
    return pl.pallas_call(
        grid_kernel,
        out_shape=(
            jax.ShapeDtypeStruct(now.shape, f32),
            jax.ShapeDtypeStruct((count_y, 3, disp.shape[1] * LANES), f32),
            jax.ShapeDtypeStruct((count_y, ID_ROWS, LANES), i32),
            jax.ShapeDtypeStruct((count_y, 3 * stripes, LANES), f32),
            jax.ShapeDtypeStruct(request.shape, f32),
        ),
        in_specs=[hbm, hbm, hbm] + [vmem] * 6 + [pl.BlockSpec(memory_space=pltpu.SMEM)],
        out_specs=(hbm, hbm, hbm, hbm, vmem),
        scratch_shapes=[
            pltpu.VMEM((3, halo_rows, LANES), f32),
            pltpu.VMEM((3, halo_rows, LANES), f32),
            pltpu.VMEM((3, rows, LANES), f32),
            pltpu.VMEM((3, rows, LANES), f32),
            pltpu.VMEM((rows, LANES), f32),
            pltpu.VMEM((2, 2, 3, planes, 8, LANES), f32),
            pltpu.VMEM((2, 2, 3, planes, 8, LANES), f32),
            pltpu.VMEM((count_x, count_y, LANES), i32),
            pltpu.VMEM((count_y, count_x, LANES), i32),
            pltpu.VMEM((count_y, count_x, LANES), i32),
            pltpu.VMEM((count_y, count_x, LANES), i32),
            pltpu.SMEM((count_y, count_x, LANES), i32),
            pltpu.VMEM((count_y, count_x, LANES), f32),
            pltpu.VMEM((count_y, count_x, LANES), f32),
            pltpu.VMEM((count_x, count_y, LANES), f32),
            pltpu.VMEM((3, disp.shape[1] * LANES), f32),
            pltpu.VMEM((count_y, ID_ROWS, LANES), i32),
            pltpu.VMEM((count_y, 3 * stripes, LANES), f32),
            pltpu.SemaphoreType.DMA((copies,)),
            pltpu.SemaphoreType.DMA((copies,)),
            pltpu.SemaphoreType.DMA((8,)),
        ],
        compiler_params=pltpu.CompilerParams(
            vmem_limit_bytes=VMEM_LIMIT, collective_id=1, has_side_effects=True
        ),
        name="grid_steps",
    )(now, before, factor, request, disp, ids, *params, live)


def gradient_signs(corner):
    lane = lax.broadcasted_iota(jnp.int32, (1, LANES), 1)
    signs = jnp.zeros((1, LANES), jnp.float32)
    for direction in range(3):
        value = 0.25 if (corner >> direction) & 1 else -0.25
        inside = (lane >= 3 * direction) & (lane < 3 * direction + 3)
        signs = jnp.where(inside, value, signs)
    return signs


def rows_of(values):
    count = values.shape[0]
    padded = jnp.concatenate(
        [values, jnp.zeros((SLOTS - count, LANES), jnp.float32)], axis=0
    )
    return padded.T


def box_kernel(
    layer_ref, slot_ref, ids_hbm, disp_ref, params_ref, reply_ref, field_in,
    out_ref, field_out, table, rows, layer_rows, reply_rows, field, counts, *rest,
):
    ids, sems, count_sem, field_sem = rest[:8], rest[8], rest[9], rest[10]
    owners, _, own = disp_ref.shape
    stripe = ids[0].shape[0] // owners
    span = ID_ROWS * LANES
    copies = []
    for part in range(owners):
        copies.append(
            pltpu.make_async_copy(
                ids_hbm.at[pl.ds(part * span + 8 * stripe, 1024)],
                counts.at[pl.ds(part * 1024, 1024)],
                count_sem.at[part],
            )
        )
        for corner in range(8):
            copies.append(
                pltpu.make_async_copy(
                    ids_hbm.at[pl.ds(part * span + corner * stripe, stripe)],
                    ids[corner].at[pl.ds(part * stripe, stripe)],
                    sems.at[part, corner],
                )
            )
    for copy in copies:
        copy.start()
    field_load = pltpu.make_async_copy(field_in, field, field_sem.at[0])
    field_load.start()

    def build(part, carry):
        for tile in range(own // LANES):
            block = disp_ref[part, :, tile * LANES : (tile + 1) * LANES]
            lines = rows_of(jnp.concatenate([block, block, block], axis=0))
            table[pl.ds(aligned(part * own + tile * LANES), LANES), 0:SLOTS] = lines
        return carry

    lax.fori_loop(0, owners, build, 0)
    field_load.wait()
    field_store = pltpu.make_async_copy(field, field_out, field_sem.at[1])
    field_store.start()
    signs = [gradient_signs(corner) for corner in range(8)]
    mine = lax.axis_index("gy")

    def live_of(part):
        count = counts[part * 1024]
        whole = count // LANES
        turn = lax.rem(mine - part + owners, owners)
        tiles = (whole + owners - 1 - turn) // owners
        partial = jnp.where(whole % owners == turn, count % LANES, 0)
        return tiles * LANES + partial


    for part in range(owners):
        for copy in copies[9 * part : 9 * part + 9]:
            copy.wait()

        def gather(chunk, carry, part=part):
            base = part * stripe + chunk * GATHER_UNROLL
            for step in range(GATHER_UNROLL):
                slot = base + step
                ends = [table[pl.ds(ids[corner][slot], 1), :] for corner in range(8)]
                spans = [ends[corner] - ends[7 - corner] for corner in range(4)]
                rows[pl.ds(slot, 1), :] = (spans[0] * signs[0] + spans[1] * signs[1]) + (
                    spans[2] * signs[2] + spans[3] * signs[3]
                )
            return carry

        lax.fori_loop(0, (live_of(part) + GATHER_UNROLL - 1) // GATHER_UNROLL, gather, 0)

    def layer_ends(chunk, carry):
        base = chunk * LAYER_UNROLL
        for step in range(LAYER_UNROLL):
            node = layer_ref[0, base + step]
            layer_rows[pl.ds(base + step, 1), :] = table[pl.ds(node, 1), :]
        return carry

    layers = layer_rows.shape[0]
    lax.fori_loop(0, layers // LAYER_UNROLL, layer_ends, 0)

    def clear(chunk, carry):
        zero = jnp.zeros((LANES, LANES), jnp.float32)
        table[pl.ds(aligned(chunk * LANES), LANES), :] = zero
        return carry

    lax.fori_loop(0, table.shape[0] // LANES, clear, 0)
    lane = lax.broadcasted_iota(jnp.int32, (1, LANES), 1)
    total = table
    tiles = stripe // LANES

    for part in range(owners):
        live = live_of(part)

        def element(tile, carry, part=part, live=live):
            start = aligned(part * stripe + tile * LANES)
            grads = rows[pl.ds(start, LANES), 0:SLOTS].T
            slope = [[grads[3 * j + i : 3 * j + i + 1] for j in range(3)] for i in range(3)]
            s00, s11, s22 = slope[0][0], slope[1][1], slope[2][2]
            s01 = 0.5 * (slope[0][1] + slope[1][0])
            s02 = 0.5 * (slope[0][2] + slope[2][0])
            s12 = 0.5 * (slope[1][2] + slope[2][1])
            trace = s00 + s11 + s22
            mean = trace / 3.0
            d00, d11, d22 = s00 - mean, s11 - mean, s22 - mean
            invariant = d00 * d00 + d11 * d11 + d22 * d22
            invariant = invariant + 2.0 * (s01 * s01 + s02 * s02 + s12 * s12)
            shear = params_ref[part, pl.ds(tile, 1), :]
            lame = params_ref[part, pl.ds(tiles + tile, 1), :]
            scale = params_ref[part, pl.ds(2 * tiles + tile, 1), :]
            softened = 2.0 * shear / (1.0 + invariant / scale)
            volume = lame * trace
            index = tile * LANES + lane

            def signed(value):
                return jnp.where(index < live, -0.25 * value, 0.0)

            p00 = signed(volume + softened * s00)
            p11 = signed(volume + softened * s11)
            p22 = signed(volume + softened * s22)
            p01, p02, p12 = signed(softened * s01), signed(softened * s02), signed(softened * s12)
            pad = jnp.zeros((GROUP - 3, LANES), jnp.float32)
            sides = [
                jnp.concatenate(column + [pad], axis=0)
                for column in ([p00, p01, p02], [p01, p11, p12], [p02, p12, p22])
            ]
            ends = []
            for corner in range(4):
                term = sides[0] if corner & 1 else -sides[0]
                term = term + sides[1] if corner & 2 else term - sides[1]
                ends.append(term - sides[2])
            ends += [-ends[7 - corner] for corner in range(4, 8)]
            rows[pl.ds(start, LANES), 0 : 8 * GROUP] = jnp.concatenate(ends, axis=0).T
            return carry

        lax.fori_loop(0, (live + LANES - 1) // LANES, element, 0)

        def scatter(chunk, carry, part=part):
            base = part * stripe + chunk * SCATTER_UNROLL
            for step in range(SCATTER_UNROLL):
                line = rows[pl.ds(base + step, 1), :]
                for corner in range(8):
                    own_lanes = slice(corner * GROUP, (corner + 1) * GROUP)
                    total[pl.ds(ids[corner][base + step], 1), own_lanes] = line[:, own_lanes]
            return carry

        lax.fori_loop(0, (live + SCATTER_UNROLL - 1) // SCATTER_UNROLL, scatter, 0)

    devices = reply_ref.shape[0]
    for position in range(LANES // SLOTS):
        values = reply_ref[...]
        if position:
            values = pltpu.roll(values, LANES - position * SLOTS, 1)
        reply_rows[position * devices : (position + 1) * devices, :] = values
    inside = lane < 3

    def layer(chunk, carry):
        base = chunk * LAYER_UNROLL
        steps = range(LAYER_UNROLL)
        nodes = [layer_ref[0, base + step] for step in steps]
        held = [total[pl.ds(node, 1), :] for node in nodes]
        for step in steps:
            reply = reply_rows[pl.ds(slot_ref[0, base + step], 1), :]
            gap = reply - layer_rows[pl.ds(base + step, 1), :]
            held[step] = held[step] + jnp.where(inside, PENALTY * gap, 0.0)
        for step in steps:
            total[pl.ds(nodes[step], 1), :] = held[step]
        return carry

    lax.fori_loop(0, layers // LAYER_UNROLL, layer, 0)

    def fold(part, carry):
        for tile in range(own // LANES):
            start = aligned(part * own + tile * LANES)
            block = total[pl.ds(start, LANES), 0 : 8 * GROUP].T
            terms = [block[corner * GROUP : corner * GROUP + GROUP] for corner in range(8)]
            while len(terms) > 1:
                terms = [a + b for a, b in zip(terms[0::2], terms[1::2])]
            out_ref[part, :, tile * LANES : (tile + 1) * LANES] = terms[0][0:3]
        return carry

    lax.fori_loop(0, owners, fold, 0)
    field_store.wait()


def box_forces(layer_ids, slot_index, ids, disp, params, replies, field):
    owners, _, own = disp.shape
    slots = params.shape[1] * LANES // 3 * owners
    layers = layer_ids.shape[1]
    smem = pl.BlockSpec(memory_space=pltpu.SMEM)
    vmem = pl.BlockSpec(memory_space=pltpu.VMEM)
    hbm = pl.BlockSpec(memory_space=pl.ANY)
    f32, i32 = jnp.float32, jnp.int32
    return pl.pallas_call(
        box_kernel,
        out_shape=(
            jax.ShapeDtypeStruct((owners, 3, own), f32),
            jax.ShapeDtypeStruct(field.shape, f32),
        ),
        in_specs=[smem, smem, hbm, vmem, vmem, vmem, hbm],
        out_specs=(vmem, hbm),
        scratch_shapes=[
            pltpu.VMEM((owners * own, LANES), f32),
            pltpu.VMEM((slots, LANES), f32),
            pltpu.VMEM((layers, LANES), f32),
            pltpu.VMEM((replies.shape[0] * (LANES // SLOTS), LANES), f32),
            pltpu.VMEM(field.shape, f32),
            pltpu.SMEM((owners * 1024,), i32),
        ]
        + [pltpu.SMEM((slots,), i32)] * 8
        + [
            pltpu.SemaphoreType.DMA((owners, 8)),
            pltpu.SemaphoreType.DMA((owners,)),
            pltpu.SemaphoreType.DMA((2,)),
        ],
        compiler_params=pltpu.CompilerParams(vmem_limit_bytes=VMEM_LIMIT),
        name="box_forces",
    )(layer_ids, slot_index, ids, disp, params, replies, field)


def sum_kernel(parts_hbm, out_ref, got, send_sems, recv_sems, local_sem):
    gx, gy = lax.axis_index("gx"), lax.axis_index("gy")
    count = lax.axis_size("gy")
    own = pltpu.make_async_copy(parts_hbm.at[gy], got.at[0], local_sem.at[0])
    own.start()
    barrier = pltpu.get_barrier_semaphore()
    for step in range(1, count):
        peer = lax.rem(gy + step, count)
        pl.semaphore_signal(barrier, inc=1, device_id=(gx, peer), device_id_type=MESH)
    pl.semaphore_wait(barrier, count - 1)
    copies = []
    for step in range(1, count):
        peer = lax.rem(gy + step, count)
        copy = pltpu.make_async_remote_copy(
            src_ref=parts_hbm.at[peer],
            dst_ref=got.at[step],
            send_sem=send_sems.at[step],
            recv_sem=recv_sems.at[step],
            device_id=(gx, peer),
            device_id_type=MESH,
        )
        copy.start()
        copies.append(copy)
    own.wait()
    for copy in copies:
        copy.wait()
    terms = [got[step] for step in range(count)]
    while len(terms) > 1:
        terms = [a + b for a, b in zip(terms[0::2], terms[1::2])]
    out_ref[...] = terms[0]


def sum_forces(parts):
    count, comps, own = parts.shape
    return pl.pallas_call(
        sum_kernel,
        out_shape=jax.ShapeDtypeStruct((comps, own), jnp.float32),
        in_specs=[pl.BlockSpec(memory_space=pl.ANY)],
        out_specs=pl.BlockSpec(memory_space=pltpu.VMEM),
        scratch_shapes=[
            pltpu.VMEM(parts.shape, jnp.float32),
            pltpu.SemaphoreType.DMA((count,)),
            pltpu.SemaphoreType.DMA((count,)),
            pltpu.SemaphoreType.DMA((1,)),
        ],
        compiler_params=pltpu.CompilerParams(
            vmem_limit_bytes=VMEM_LIMIT, collective_id=2, has_side_effects=True
        ),
        name="sum_forces",
    )(parts)


def tiled_rows(field):
    lead, (rows, cols) = field.shape[:-2], field.shape[-2:]
    tiles = field.reshape(lead + (rows // 8, 8, cols // LANES, LANES))
    tiles = jnp.swapaxes(tiles, -3, -2)
    return tiles.reshape(lead[:-1] + (-1, LANES))


def untiled_rows(values, shape):
    rows, cols = shape[-2:]
    tiles = values.reshape(shape[:-2] + (rows // 8, cols // LANES, 8, LANES))
    return jnp.swapaxes(tiles, -3, -2).reshape(shape)


def on_device(
    grid_now,
    grid_before,
    wave_factor,
    layer_owner,
    layer_cell,
    box_now,
    box_before,
    node_mass,
    corner_nodes,
    live_counts,
    shear_modulus,
    lame_lambda,
    strain_scale,
    layer_nodes,
):
    count_x, count_y = lax.axis_size("gx"), lax.axis_size("gy")
    devices = count_x * count_y
    own_disp = box_now.reshape(3, -1)

    request, slot_index = rank_requests(
        layer_owner.reshape(1, -1), layer_cell.reshape(1, -1), devices
    )
    lines = (-1, LANES)

    after, all_disp, all_ids, all_params, replies = grid_steps(
        tiled_rows(grid_now),
        tiled_rows(grid_before),
        tiled_rows(wave_factor),
        request.reshape(count_x, count_y, LANES),
        box_now.reshape(3, -1, 1, LANES),
        corner_nodes.reshape(8, -1, LANES),
        [values.reshape(lines) for values in (shear_modulus, lame_lambda, strain_scale)],
        live_counts,
        count_x,
        count_y,
    )
    node_term, after = box_forces(
        layer_nodes,
        slot_index,
        all_ids.reshape(-1),
        all_disp,
        all_params,
        replies.reshape(devices, LANES),
        after,
    )
    summed = sum_forces(node_term)
    box_after = 2.0 * own_disp - box_before.reshape(3, -1) + STEP_SQUARE / node_mass * summed
    return (untiled_rows(after, grid_now.shape), box_after.reshape(box_now.shape))


def solution(mesh):
    return jax.shard_map(
        on_device,
        mesh=mesh,
        in_specs=(
            P(None, "gx", "gy", None),
            P(None, "gx", "gy", None),
            P("gx", "gy", None),
            P("gx", "gy", None),
            P("gx", "gy"),
            P(None, "gx", "gy"),
            P(None, "gx", "gy"),
            P("gx", "gy"),
            P(None, "gx", "gy"),
            P("gx", "gy"),
            P("gx", "gy"),
            P("gx", "gy"),
            P("gx", "gy"),
            P("gx", "gy"),
        ),
        out_specs=(P(None, "gx", "gy", None), P(None, "gx", "gy")),
        check_vma=False,
    )
```

```python
import jax
import jax.numpy as jnp
from jax import lax
from jax.experimental import pallas as pl
from jax.experimental.pallas import tpu as pltpu
from jax.sharding import PartitionSpec as P

PENALTY = 2.0
STEP_SQUARE = 0.25
NEAR = 16.0 / 12.0
FAR = -1.0 / 12.0
LANES = 128
SLOTS = 16
ID_ROWS = 72
PLANE = 128
VMEM_LIMIT = 58 * 2**20
GATHER_UNROLL = 32
SCATTER_UNROLL = 16
LAYER_UNROLL = 16
GROUP = 8
MESH = pl.DeviceIdType.MESH


def aligned(start, unit=LANES):
    return pl.multiple_of(start, unit)


def rank_kernel(owner_ref, cell_ref, request_out, slot_out):
    devices, layers = request_out.shape[0], owner_ref.shape[1]
    row = lax.broadcasted_iota(jnp.int32, (devices, layers), 0)
    owner, cell = owner_ref[...], cell_ref[...]
    found = row == owner
    matches = jnp.where(found, 1.0, 0.0).astype(jnp.bfloat16)
    first = lax.broadcasted_iota(jnp.int32, (layers, layers), 0)
    second = lax.broadcasted_iota(jnp.int32, (layers, layers), 1)
    earlier = jnp.where(first < second, 1.0, 0.0).astype(jnp.bfloat16)
    before = jnp.dot(matches, earlier, preferred_element_type=jnp.float32)
    position = jnp.sum(jnp.where(found, before, 0.0), axis=0, keepdims=True).astype(jnp.int32)
    placed = row == position
    request = jnp.zeros((devices, devices), jnp.int32)
    for shift in (0, 6, 12):
        digit = ((cell >> shift) & 63).astype(jnp.float32)
        digits = jnp.where(placed, digit, 0.0).astype(jnp.bfloat16)
        part = lax.dot_general(
            matches, digits, (((1,), (1,)), ((), ())), preferred_element_type=jnp.float32
        )
        request = request + (part.astype(jnp.int32) << shift)
    request_out[...] = request
    slot_out[...] = position * devices + owner


def rank_requests(owners, cells, devices):
    vmem = pl.BlockSpec(memory_space=pltpu.VMEM)
    return pl.pallas_call(
        rank_kernel,
        out_shape=(
            jax.ShapeDtypeStruct((devices, LANES), jnp.int32),
            jax.ShapeDtypeStruct(owners.shape, jnp.int32),
        ),
        in_specs=[vmem, vmem],
        out_specs=(vmem, vmem),
        name="rank_requests",
    )(owners, cells)


def wave_plane(comp, index, now, before, factor, out, out_shift):
    start = aligned((index + 2) * PLANE)

    def block(offset, group, tile):
        return now[comp, pl.ds(start + offset * PLANE + (group * 4 + tile) * 8, 8), :]

    sub = lax.broadcasted_iota(jnp.int32, (8, LANES), 0)
    lane = lax.broadcasted_iota(jnp.int32, (8, LANES), 1)
    zero = jnp.zeros((8, LANES), jnp.float32)
    here = [[block(0, group, tile) for tile in range(4)] for group in range(4)]

    def neighbours(values, axis, count, position):
        sums = []
        for distance in (1, 2):
            ahead = [pltpu.roll(value, distance, axis) for value in values]
            behind = [pltpu.roll(value, count - distance, axis) for value in values]
            rows = []
            for spot in range(4):
                low = ahead[spot - 1] if spot > 0 else zero
                high = behind[spot + 1] if spot < 3 else zero
                rows.append(
                    jnp.where(position < distance, low, ahead[spot])
                    + jnp.where(position >= count - distance, high, behind[spot])
                )
            sums.append(rows)
        return sums

    along_y = [neighbours([here[g][t] for g in range(4)], 0, 8, sub) for t in range(4)]
    along_z = [neighbours(here[g], 1, LANES, lane) for g in range(4)]
    for group in range(4):
        for tile in range(4):
            row = (group * 4 + tile) * 8
            near = block(-1, group, tile) + block(1, group, tile)
            far = block(-2, group, tile) + block(2, group, tile)
            near = near + (along_y[tile][0][group] + along_z[group][0][tile])
            far = far + (along_y[tile][1][group] + along_z[group][1][tile])
            centre = here[group][tile]
            laplace = NEAR * near + FAR * far - 7.5 * centre
            place = pl.ds(aligned(index * PLANE) + row, 8)
            result = 2.0 * centre - before[comp, pl.ds(aligned(before_start(before, index)) + row, 8), :]
            out[comp, pl.ds(aligned((index + out_shift) * PLANE) + row, 8), :] = (
                result + factor[place, :] * laplace
            )


def before_start(before, index):
    shift = 2 if before.shape[1] == 20 * PLANE else 0
    return (index + shift) * PLANE


def y_edges(comp, index, source, low_out, high_out):
    start = aligned((index + 2) * PLANE)
    for tile in range(4):
        first = source[comp, pl.ds(start + tile * 8, 8), :]
        last = source[comp, pl.ds(start + 96 + tile * 8, 8), :]
        low_out[comp, index, 2 * tile : 2 * tile + 2, :] = first[0:2]
        high_out[comp, index, 2 * tile : 2 * tile + 2, :] = last[6:8]


def y_corrections(comp, index, low, high, low_weight, high_weight, factor, out, out_shift):
    sub = lax.broadcasted_iota(jnp.int32, (8, LANES), 0)
    start = aligned((index + out_shift) * PLANE)
    here = aligned(index * PLANE)
    lows = low[comp, index] * low_weight
    highs = high[comp, index] * high_weight
    for tile in range(4):
        far_row, near_row = lows[2 * tile : 2 * tile + 1], lows[2 * tile + 1 : 2 * tile + 2]
        term = jnp.where(
            sub == 0, NEAR * near_row + FAR * far_row, jnp.where(sub == 1, FAR * near_row, 0.0)
        )
        place = pl.ds(start + tile * 8, 8)
        out[comp, place, :] = out[comp, place, :] + factor[pl.ds(here + tile * 8, 8), :] * term
        near_row, far_row = highs[2 * tile : 2 * tile + 1], highs[2 * tile + 1 : 2 * tile + 2]
        term = jnp.where(
            sub == 7, NEAR * near_row + FAR * far_row, jnp.where(sub == 6, FAR * near_row, 0.0)
        )
        place = pl.ds(start + 96 + tile * 8, 8)
        out[comp, place, :] = out[comp, place, :] + factor[pl.ds(here + 96 + tile * 8, 8), :] * term


def grid_kernel(
    now_hbm, before_hbm, factor_hbm, request, disp_raw, ids_raw, shear_raw, lame_raw, scale_raw, live,
    after_hbm, disp_all, ids_all, params_all, reply_out,
    now, mid, after, before, factor, y_sent, y_got, asked_x, asked_t, asked_y, rows_vmem,
    rows_smem, found, found_x, found_t, disp_own, ids_own, params_own, send_sems, recv_sems, local_sems,
    store_sems,
):
    gx, gy = lax.axis_index("gx"), lax.axis_index("gy")
    count_x, count_y = lax.axis_size("gx"), lax.axis_size("gy")
    planes = factor.shape[0] // PLANE
    edge = 2 * PLANE
    inside = pl.ds(edge, planes * PLANE)

    loads = [
        pltpu.make_async_copy(now_hbm, now.at[:, inside, :], local_sems.at[0]),
        pltpu.make_async_copy(before_hbm, before, local_sems.at[1]),
        pltpu.make_async_copy(factor_hbm, factor, local_sems.at[2]),
    ]
    for load in loads:
        load.start()

    barrier = pltpu.get_barrier_semaphore()
    for step in range(1, count_x):
        peer = lax.rem(gx + step, count_x)
        pl.semaphore_signal(barrier, inc=1, device_id=(peer, gy), device_id_type=MESH)
    for step in range(1, count_y):
        peer = lax.rem(gy + step, count_y)
        pl.semaphore_signal(barrier, inc=1, device_id=(gx, peer), device_id_type=MESH)
    pl.semaphore_wait(barrier, count_x + count_y - 2)

    used = [0]

    def send(source, target, device):
        slot = used[0]
        used[0] += 1
        copy = pltpu.make_async_remote_copy(
            src_ref=source,
            dst_ref=target,
            send_sem=send_sems.at[slot],
            recv_sem=recv_sems.at[slot],
            device_id=device,
            device_id_type=MESH,
        )
        copy.start()
        return copy

    right, left = lax.rem(gx + 1, count_x), lax.rem(gx + count_x - 1, count_x)
    upper, lower = lax.rem(gy + 1, count_y), lax.rem(gy + count_y - 1, count_y)
    top = (planes - 2) * PLANE

    def x_halo(source, shift, target, comp):
        return [
            send(
                source.at[comp, pl.ds(top + shift, edge), :],
                target.at[comp, pl.ds(0, edge), :],
                (right, gy),
            ),
            send(
                source.at[comp, pl.ds(shift, edge), :],
                target.at[comp, pl.ds(edge + planes * PLANE, edge), :],
                (left, gy),
            ),
        ]

    def y_halo(step, comp):
        return [
            send(y_sent.at[step, 1, comp], y_got.at[step, 0, comp], (gx, upper)),
            send(y_sent.at[step, 0, comp], y_got.at[step, 1, comp], (gx, lower)),
        ]

    def each_plane(comp, ranges, body):
        for low, high in ranges:
            lax.fori_loop(low, high, lambda index, c: (body(comp, index), c)[1], 0)

    def edges(step, source, comp):
        each_plane(
            comp,
            [(0, planes)],
            lambda comp, index: y_edges(comp, index, source, y_sent.at[step, 0], y_sent.at[step, 1]),
        )

    def clear_outside(target, comp):
        @pl.when(gx == 0)
        def _():
            target[comp, 0:edge, :] = jnp.zeros((edge, LANES), jnp.float32)

        @pl.when(gx == count_x - 1)
        def _():
            target[comp, edge + planes * PLANE :, :] = jnp.zeros((edge, LANES), jnp.float32)

    low_weight = jnp.where(gy == 0, 0.0, 1.0).astype(jnp.float32)
    high_weight = jnp.where(gy == count_y - 1, 0.0, 1.0).astype(jnp.float32)

    first_x = [x_halo(now_hbm, 0, now, comp) for comp in range(3)]
    asks = []
    for step in range(1, count_x):
        peer = lax.rem(gx + step, count_x)
        asks.append(send(request.at[peer], asked_x.at[gx], (peer, gy)))
    asked_x[gx] = request[gx]
    loads[0].wait()
    first_y = []
    for comp in range(3):
        edges(0, now, comp)
        first_y.append(y_halo(0, comp))
    for comp in range(3):
        for tile in range(disp_raw.shape[1]):
            disp_own[comp : comp + 1, tile * LANES : (tile + 1) * LANES] = disp_raw[comp, tile]
    stripes = ids_raw.shape[1] // count_y
    for turn in range(count_y):
        every = pl.ds(turn, stripes, stride=count_y)
        for corner in range(8):
            here = slice(corner * stripes, (corner + 1) * stripes)
            ids_own[turn, here, :] = ids_raw[corner, every, :]
        ids_own[turn, 8 * stripes :, :] = jnp.full((8, LANES), live[0, 0], jnp.int32)
        for index, raw in enumerate((shear_raw, lame_raw, scale_raw)):
            here = slice(index * stripes, (index + 1) * stripes)
            params_own[turn, here, :] = raw[every, :]
    bulk = []
    for step in range(1, count_y):
        peer = lax.rem(gy + step, count_y)
        bulk.append(send(disp_own, disp_all.at[gy], (gx, peer)))
        bulk.append(send(ids_own.at[step], ids_all.at[gy], (gx, peer)))
        bulk.append(send(params_own.at[step], params_all.at[gy], (gx, peer)))
    own = [
        pltpu.make_async_copy(disp_own, disp_all.at[gy], local_sems.at[3]),
        pltpu.make_async_copy(ids_own.at[0], ids_all.at[gy], local_sems.at[4]),
        pltpu.make_async_copy(params_own.at[0], params_all.at[gy], local_sems.at[5]),
    ]
    for copy in own:
        copy.start()
    loads[1].wait()
    loads[2].wait()

    def step_of(source, previous, target, shift):
        return lambda comp, index: wave_plane(comp, index, source, previous, factor, target, shift)

    def fix(step, target, shift, comp):
        each_plane(
            comp,
            [(0, planes)],
            lambda comp, index: y_corrections(
                comp, index, y_got.at[step, 0], y_got.at[step, 1], low_weight, high_weight,
                factor, target, shift,
            ),
        )

    inner, outer = [(2, planes - 2)], [(0, 2), (planes - 2, planes)]
    first = step_of(now, before, mid, 2)
    second = step_of(mid, now, after, 0)
    for comp in range(3):
        each_plane(comp, inner, first)
    second_x, second_y, passes = [], [], []
    for comp in range(3):
        for copy in first_x[comp]:
            copy.wait()
        clear_outside(now, comp)
        each_plane(comp, outer, first)
        for copy in first_y[comp]:
            copy.wait()
        fix(0, mid, 2, comp)
        second_x.append(x_halo(mid, edge, mid, comp))
        edges(1, mid, comp)
        second_y.append(y_halo(1, comp))
        if comp == 0:
            for copy in asks:
                copy.wait()
            for peer in range(count_y):
                asked_t[peer] = asked_x[:, peer, :]
            for step in range(1, count_y):
                peer = lax.rem(gy + step, count_y)
                passes.append(send(asked_t.at[peer], asked_y.at[gy], (gx, peer)))
            asked_y[gy] = asked_t[gy]
        each_plane(comp, inner, second)
    for copy in passes:
        copy.wait()
    cell = asked_y[...]
    plane, row, col = cell >> 14, (cell >> 9) & 31, cell & 511
    rows_vmem[...] = (((plane * 4 + (row >> 3)) * 4 + (col >> 7)) * 8 + (row & 7)) * LANES + (
        col & (LANES - 1)
    )
    to_smem = pltpu.make_async_copy(rows_vmem, rows_smem, local_sems.at[6])
    to_smem.start()
    stores = []
    for comp in range(3):
        for copy in second_x[comp]:
            copy.wait()
        clear_outside(mid, comp)
        each_plane(comp, outer, second)
        for copy in second_y[comp]:
            copy.wait()
        fix(1, after, 0, comp)
        store = pltpu.make_async_copy(after.at[comp], after_hbm.at[comp], store_sems.at[comp])
        store.start()
        stores.append(store)
    to_smem.wait()

    lane = lax.broadcasted_iota(jnp.int32, (1, LANES), 1)
    capacity = LANES // SLOTS

    unroll = 8

    def find(part):
        def run(chunk, carry):
            for step in range(unroll):
                source = chunk * unroll + step
                held = jnp.zeros((1, LANES), jnp.float32)
                for position in range(capacity):
                    place = rows_smem[part, source, position]
                    line = place >> 7
                    for comp in range(3):
                        spot = position * SLOTS + comp
                        values = after[comp, pl.ds(line, 1), :]
                        shift = (spot - place) & (LANES - 1)
                        held = jnp.where(lane == spot, pltpu.roll(values, shift, 1), held)
                found[part, pl.ds(source, 1), :] = held
            return carry

        lax.fori_loop(0, count_x // unroll, run, 0)

    answers = []
    for step in range(1, count_y):
        peer = lax.rem(gy + step, count_y)
        find(peer)
        answers.append(send(found.at[peer], found_x.at[gy], (gx, peer)))
    find(gy)
    found_x[gy] = found[gy]
    for copy in answers:
        copy.wait()
    for peer in range(count_x):
        found_t[peer] = found_x[:, peer, :]
    finals = []
    for step in range(1, count_x):
        peer = lax.rem(gx + step, count_x)
        finals.append(send(found_t.at[peer], reply_out.at[gx], (peer, gy)))
    reply_out[gx] = found_t[gx]
    for copy in finals + bulk + own:
        copy.wait()
    for store in stores:
        store.wait()


def grid_steps(now, before, factor, request, disp, ids, params, live, count_x, count_y):
    rows = factor.shape[0]
    f32, i32 = jnp.float32, jnp.int32
    hbm = pl.BlockSpec(memory_space=pl.ANY)
    vmem = pl.BlockSpec(memory_space=pltpu.VMEM)
    halo_rows = rows + 4 * PLANE
    copies = 24 + 3 * (count_y - 1) + 2 * (count_x - 1) + 2 * (count_y - 1)
    planes = rows // PLANE
    stripes = ids.shape[1] // count_y
    return pl.pallas_call(
        grid_kernel,
        out_shape=(
            jax.ShapeDtypeStruct(now.shape, f32),
            jax.ShapeDtypeStruct((count_y, 3, disp.shape[1] * LANES), f32),
            jax.ShapeDtypeStruct((count_y, ID_ROWS, LANES), i32),
            jax.ShapeDtypeStruct((count_y, 3 * stripes, LANES), f32),
            jax.ShapeDtypeStruct(request.shape, f32),
        ),
        in_specs=[hbm, hbm, hbm] + [vmem] * 6 + [pl.BlockSpec(memory_space=pltpu.SMEM)],
        out_specs=(hbm, hbm, hbm, hbm, vmem),
        scratch_shapes=[
            pltpu.VMEM((3, halo_rows, LANES), f32),
            pltpu.VMEM((3, halo_rows, LANES), f32),
            pltpu.VMEM((3, rows, LANES), f32),
            pltpu.VMEM((3, rows, LANES), f32),
            pltpu.VMEM((rows, LANES), f32),
            pltpu.VMEM((2, 2, 3, planes, 8, LANES), f32),
            pltpu.VMEM((2, 2, 3, planes, 8, LANES), f32),
            pltpu.VMEM((count_x, count_y, LANES), i32),
            pltpu.VMEM((count_y, count_x, LANES), i32),
            pltpu.VMEM((count_y, count_x, LANES), i32),
            pltpu.VMEM((count_y, count_x, LANES), i32),
            pltpu.SMEM((count_y, count_x, LANES), i32),
            pltpu.VMEM((count_y, count_x, LANES), f32),
            pltpu.VMEM((count_y, count_x, LANES), f32),
            pltpu.VMEM((count_x, count_y, LANES), f32),
            pltpu.VMEM((3, disp.shape[1] * LANES), f32),
            pltpu.VMEM((count_y, ID_ROWS, LANES), i32),
            pltpu.VMEM((count_y, 3 * stripes, LANES), f32),
            pltpu.SemaphoreType.DMA((copies,)),
            pltpu.SemaphoreType.DMA((copies,)),
            pltpu.SemaphoreType.DMA((8,)),
            pltpu.SemaphoreType.DMA((3,)),
        ],
        compiler_params=pltpu.CompilerParams(
            vmem_limit_bytes=VMEM_LIMIT, collective_id=1, has_side_effects=True
        ),
        name="grid_steps",
    )(now, before, factor, request, disp, ids, *params, live)


def gradient_signs(corner):
    lane = lax.broadcasted_iota(jnp.int32, (1, LANES), 1)
    signs = jnp.zeros((1, LANES), jnp.float32)
    for direction in range(3):
        value = 0.25 if (corner >> direction) & 1 else -0.25
        inside = (lane >= 3 * direction) & (lane < 3 * direction + 3)
        signs = jnp.where(inside, value, signs)
    return signs


def rows_of(values):
    count = values.shape[0]
    padded = jnp.concatenate(
        [values, jnp.zeros((SLOTS - count, LANES), jnp.float32)], axis=0
    )
    return padded.T


def box_kernel(
    layer_ref, slot_ref, ids_hbm, disp_ref, params_ref, reply_ref, field_in,
    out_ref, field_out, table, rows, layer_rows, reply_rows, field, counts, *rest,
):
    ids, sems, count_sem, field_sem = rest[:8], rest[8], rest[9], rest[10]
    owners, _, own = disp_ref.shape
    stripe = ids[0].shape[0] // owners
    span = ID_ROWS * LANES
    copies = []
    for part in range(owners):
        copies.append(
            pltpu.make_async_copy(
                ids_hbm.at[pl.ds(part * span + 8 * stripe, 1024)],
                counts.at[pl.ds(part * 1024, 1024)],
                count_sem.at[part],
            )
        )
        for corner in range(8):
            copies.append(
                pltpu.make_async_copy(
                    ids_hbm.at[pl.ds(part * span + corner * stripe, stripe)],
                    ids[corner].at[pl.ds(part * stripe, stripe)],
                    sems.at[part, corner],
                )
            )
    for copy in copies:
        copy.start()
    field_load = pltpu.make_async_copy(field_in, field, field_sem.at[0])
    field_load.start()

    def build(part, carry):
        for tile in range(own // LANES):
            block = disp_ref[part, :, tile * LANES : (tile + 1) * LANES]
            lines = rows_of(jnp.concatenate([block, block, block], axis=0))
            table[pl.ds(aligned(part * own + tile * LANES), LANES), 0:SLOTS] = lines
        return carry

    lax.fori_loop(0, owners, build, 0)
    field_load.wait()
    field_store = pltpu.make_async_copy(field, field_out, field_sem.at[1])
    field_store.start()
    signs = [gradient_signs(corner) for corner in range(8)]
    mine = lax.axis_index("gy")

    def live_of(part):
        count = counts[part * 1024]
        whole = count // LANES
        turn = lax.rem(mine - part + owners, owners)
        tiles = (whole + owners - 1 - turn) // owners
        partial = jnp.where(whole % owners == turn, count % LANES, 0)
        return tiles * LANES + partial


    for part in range(owners):
        for copy in copies[9 * part : 9 * part + 9]:
            copy.wait()

        def gather(chunk, carry, part=part):
            base = part * stripe + chunk * GATHER_UNROLL
            for step in range(GATHER_UNROLL):
                slot = base + step
                ends = [table[pl.ds(ids[corner][slot], 1), :] for corner in range(8)]
                spans = [ends[corner] - ends[7 - corner] for corner in range(4)]
                rows[pl.ds(slot, 1), :] = (spans[0] * signs[0] + spans[1] * signs[1]) + (
                    spans[2] * signs[2] + spans[3] * signs[3]
                )
            return carry

        lax.fori_loop(0, (live_of(part) + GATHER_UNROLL - 1) // GATHER_UNROLL, gather, 0)

    def layer_ends(chunk, carry):
        base = chunk * LAYER_UNROLL
        for step in range(LAYER_UNROLL):
            node = layer_ref[0, base + step]
            layer_rows[pl.ds(base + step, 1), :] = table[pl.ds(node, 1), :]
        return carry

    layers = layer_rows.shape[0]
    lax.fori_loop(0, layers // LAYER_UNROLL, layer_ends, 0)

    def clear(chunk, carry):
        zero = jnp.zeros((LANES, LANES), jnp.float32)
        table[pl.ds(aligned(chunk * LANES), LANES), :] = zero
        return carry

    lax.fori_loop(0, table.shape[0] // LANES, clear, 0)
    lane = lax.broadcasted_iota(jnp.int32, (1, LANES), 1)
    total = table
    tiles = stripe // LANES

    for part in range(owners):
        live = live_of(part)

        def element(tile, carry, part=part, live=live):
            start = aligned(part * stripe + tile * LANES)
            grads = rows[pl.ds(start, LANES), 0:SLOTS].T
            slope = [[grads[3 * j + i : 3 * j + i + 1] for j in range(3)] for i in range(3)]
            s00, s11, s22 = slope[0][0], slope[1][1], slope[2][2]
            s01 = 0.5 * (slope[0][1] + slope[1][0])
            s02 = 0.5 * (slope[0][2] + slope[2][0])
            s12 = 0.5 * (slope[1][2] + slope[2][1])
            trace = s00 + s11 + s22
            mean = trace / 3.0
            d00, d11, d22 = s00 - mean, s11 - mean, s22 - mean
            invariant = d00 * d00 + d11 * d11 + d22 * d22
            invariant = invariant + 2.0 * (s01 * s01 + s02 * s02 + s12 * s12)
            shear = params_ref[part, pl.ds(tile, 1), :]
            lame = params_ref[part, pl.ds(tiles + tile, 1), :]
            scale = params_ref[part, pl.ds(2 * tiles + tile, 1), :]
            softened = 2.0 * shear / (1.0 + invariant / scale)
            volume = lame * trace
            index = tile * LANES + lane

            def signed(value):
                return jnp.where(index < live, -0.25 * value, 0.0)

            p00 = signed(volume + softened * s00)
            p11 = signed(volume + softened * s11)
            p22 = signed(volume + softened * s22)
            p01, p02, p12 = signed(softened * s01), signed(softened * s02), signed(softened * s12)
            pad = jnp.zeros((GROUP - 3, LANES), jnp.float32)
            sides = [
                jnp.concatenate(column + [pad], axis=0)
                for column in ([p00, p01, p02], [p01, p11, p12], [p02, p12, p22])
            ]
            ends = []
            for corner in range(4):
                term = sides[0] if corner & 1 else -sides[0]
                term = term + sides[1] if corner & 2 else term - sides[1]
                ends.append(term - sides[2])
            ends += [-ends[7 - corner] for corner in range(4, 8)]
            rows[pl.ds(start, LANES), 0 : 8 * GROUP] = jnp.concatenate(ends, axis=0).T
            return carry

        lax.fori_loop(0, (live + LANES - 1) // LANES, element, 0)

        def scatter(chunk, carry, part=part):
            base = part * stripe + chunk * SCATTER_UNROLL
            for step in range(SCATTER_UNROLL):
                line = rows[pl.ds(base + step, 1), :]
                for corner in range(8):
                    own_lanes = slice(corner * GROUP, (corner + 1) * GROUP)
                    total[pl.ds(ids[corner][base + step], 1), own_lanes] = line[:, own_lanes]
            return carry

        lax.fori_loop(0, (live + SCATTER_UNROLL - 1) // SCATTER_UNROLL, scatter, 0)

    devices = reply_ref.shape[0]
    for position in range(LANES // SLOTS):
        values = reply_ref[...]
        if position:
            values = pltpu.roll(values, LANES - position * SLOTS, 1)
        reply_rows[position * devices : (position + 1) * devices, :] = values
    inside = lane < 3

    def layer(chunk, carry):
        base = chunk * LAYER_UNROLL
        steps = range(LAYER_UNROLL)
        nodes = [layer_ref[0, base + step] for step in steps]
        held = [total[pl.ds(node, 1), :] for node in nodes]
        for step in steps:
            reply = reply_rows[pl.ds(slot_ref[0, base + step], 1), :]
            gap = reply - layer_rows[pl.ds(base + step, 1), :]
            held[step] = held[step] + jnp.where(inside, PENALTY * gap, 0.0)
        for step in steps:
            total[pl.ds(nodes[step], 1), :] = held[step]
        return carry

    lax.fori_loop(0, layers // LAYER_UNROLL, layer, 0)

    def fold(part, carry):
        for tile in range(own // LANES):
            start = aligned(part * own + tile * LANES)
            block = total[pl.ds(start, LANES), 0 : 8 * GROUP].T
            terms = [block[corner * GROUP : corner * GROUP + GROUP] for corner in range(8)]
            while len(terms) > 1:
                terms = [a + b for a, b in zip(terms[0::2], terms[1::2])]
            for comp in range(3):
                line = comp * (own // LANES) + tile
                out_ref[part, line : line + 1, :] = terms[0][comp : comp + 1]
        return carry

    lax.fori_loop(0, owners, fold, 0)
    field_store.wait()


def box_forces(layer_ids, slot_index, ids, disp, params, replies, field):
    owners, _, own = disp.shape
    slots = params.shape[1] * LANES // 3 * owners
    layers = layer_ids.shape[1]
    smem = pl.BlockSpec(memory_space=pltpu.SMEM)
    vmem = pl.BlockSpec(memory_space=pltpu.VMEM)
    hbm = pl.BlockSpec(memory_space=pl.ANY)
    f32, i32 = jnp.float32, jnp.int32
    return pl.pallas_call(
        box_kernel,
        out_shape=(
            jax.ShapeDtypeStruct((owners, 3 * own // LANES, LANES), f32),
            jax.ShapeDtypeStruct(field.shape, f32),
        ),
        in_specs=[smem, smem, hbm, vmem, vmem, vmem, hbm],
        out_specs=(vmem, hbm),
        scratch_shapes=[
            pltpu.VMEM((owners * own, LANES), f32),
            pltpu.VMEM((slots, LANES), f32),
            pltpu.VMEM((layers, LANES), f32),
            pltpu.VMEM((replies.shape[0] * (LANES // SLOTS), LANES), f32),
            pltpu.VMEM(field.shape, f32),
            pltpu.SMEM((owners * 1024,), i32),
        ]
        + [pltpu.SMEM((slots,), i32)] * 8
        + [
            pltpu.SemaphoreType.DMA((owners, 8)),
            pltpu.SemaphoreType.DMA((owners,)),
            pltpu.SemaphoreType.DMA((2,)),
        ],
        compiler_params=pltpu.CompilerParams(vmem_limit_bytes=VMEM_LIMIT),
        name="box_forces",
    )(layer_ids, slot_index, ids, disp, params, replies, field)


def sum_kernel(
    parts_hbm, out_ref, mine, near, sums, far, send_sems, recv_sems, local_sem
):
    gx, gy = lax.axis_index("gx"), lax.axis_index("gy")
    pairs = lax.axis_size("gy") // 2
    side, place = lax.rem(gy, 2), gy // 2
    other = 2 * place + 1 - side
    load = pltpu.make_async_copy(parts_hbm.at[:, side], mine, local_sem.at[0])
    load.start()
    barrier = pltpu.get_barrier_semaphore()
    pl.semaphore_signal(barrier, inc=1, device_id=(gx, other), device_id_type=MESH)
    for step in range(1, pairs):
        peer = 2 * lax.rem(place + step, pairs) + side
        pl.semaphore_signal(barrier, inc=1, device_id=(gx, peer), device_id_type=MESH)
    pl.semaphore_wait(barrier, pairs)
    swap = pltpu.make_async_remote_copy(
        src_ref=parts_hbm.at[:, 1 - side],
        dst_ref=near,
        send_sem=send_sems.at[0],
        recv_sem=recv_sems.at[0],
        device_id=(gx, other),
        device_id_type=MESH,
    )
    swap.start()
    load.wait()
    swap.wait()
    copies = []
    for step in range(1, pairs):
        target = lax.rem(place + step, pairs)
        sums[step] = mine[target] + near[target]
        copy = pltpu.make_async_remote_copy(
            src_ref=sums.at[step],
            dst_ref=far.at[step],
            send_sem=send_sems.at[step],
            recv_sem=recv_sems.at[step],
            device_id=(gx, 2 * target + side),
            device_id_type=MESH,
        )
        copy.start()
        copies.append(copy)
    total = mine[place] + near[place]
    for step, copy in enumerate(copies, 1):
        copy.wait()
        total = total + far[step]
    out_ref[...] = total


def sum_forces(parts):
    count, rows, _ = parts.shape
    block = pltpu.VMEM((count // 2, rows, LANES), jnp.float32)
    return pl.pallas_call(
        sum_kernel,
        out_shape=jax.ShapeDtypeStruct((rows, LANES), jnp.float32),
        in_specs=[pl.BlockSpec(memory_space=pl.ANY)],
        out_specs=pl.BlockSpec(memory_space=pltpu.VMEM),
        scratch_shapes=[
            block,
            block,
            block,
            block,
            pltpu.SemaphoreType.DMA((count // 2,)),
            pltpu.SemaphoreType.DMA((count // 2,)),
            pltpu.SemaphoreType.DMA((1,)),
        ],
        compiler_params=pltpu.CompilerParams(
            vmem_limit_bytes=VMEM_LIMIT, collective_id=2, has_side_effects=True
        ),
        name="sum_forces",
    )(parts.reshape(count // 2, 2, rows, LANES))


def tiled_rows(field):
    lead, (rows, cols) = field.shape[:-2], field.shape[-2:]
    tiles = field.reshape(lead + (rows // 8, 8, cols // LANES, LANES))
    tiles = jnp.swapaxes(tiles, -3, -2)
    return tiles.reshape(lead[:-1] + (-1, LANES))


def untiled_rows(values, shape):
    rows, cols = shape[-2:]
    tiles = values.reshape(shape[:-2] + (rows // 8, cols // LANES, 8, LANES))
    return jnp.swapaxes(tiles, -3, -2).reshape(shape)


def on_device(
    grid_now,
    grid_before,
    wave_factor,
    layer_owner,
    layer_cell,
    box_now,
    box_before,
    node_mass,
    corner_nodes,
    live_counts,
    shear_modulus,
    lame_lambda,
    strain_scale,
    layer_nodes,
):
    count_x, count_y = lax.axis_size("gx"), lax.axis_size("gy")
    devices = count_x * count_y
    own_disp = box_now.reshape(3, -1)

    request, slot_index = rank_requests(
        layer_owner.reshape(1, -1), layer_cell.reshape(1, -1), devices
    )
    lines = (-1, LANES)

    after, all_disp, all_ids, all_params, replies = grid_steps(
        tiled_rows(grid_now),
        tiled_rows(grid_before),
        tiled_rows(wave_factor),
        request.reshape(count_x, count_y, LANES),
        box_now.reshape(3, -1, 1, LANES),
        corner_nodes.reshape(8, -1, LANES),
        [values.reshape(lines) for values in (shear_modulus, lame_lambda, strain_scale)],
        live_counts,
        count_x,
        count_y,
    )
    node_term, after = box_forces(
        layer_nodes,
        slot_index,
        all_ids.reshape(-1),
        all_disp,
        all_params,
        replies.reshape(devices, LANES),
        after,
    )
    summed = sum_forces(node_term).reshape(own_disp.shape)
    box_after = 2.0 * own_disp - box_before.reshape(3, -1) + STEP_SQUARE / node_mass * summed
    return (untiled_rows(after, grid_now.shape), box_after.reshape(box_now.shape))


def solution(mesh):
    return jax.shard_map(
        on_device,
        mesh=mesh,
        in_specs=(
            P(None, "gx", "gy", None),
            P(None, "gx", "gy", None),
            P("gx", "gy", None),
            P("gx", "gy", None),
            P("gx", "gy"),
            P(None, "gx", "gy"),
            P(None, "gx", "gy"),
            P("gx", "gy"),
            P(None, "gx", "gy"),
            P("gx", "gy"),
            P("gx", "gy"),
            P("gx", "gy"),
            P("gx", "gy"),
            P("gx", "gy"),
        ),
        out_specs=(P(None, "gx", "gy", None), P(None, "gx", "gy")),
        check_vma=False,
    )
```

```python
import jax
import jax.numpy as jnp
from jax import lax
from jax.experimental import pallas as pl
from jax.experimental.pallas import tpu as pltpu
from jax.sharding import PartitionSpec as P

PENALTY = 2.0
STEP_SQUARE = 0.25
NEAR = 16.0 / 12.0
FAR = -1.0 / 12.0
LANES = 128
SLOTS = 16
ID_ROWS = 72
PLANE = 128
VMEM_LIMIT = 58 * 2**20
GATHER_UNROLL = 32
SCATTER_UNROLL = 32
LAYER_UNROLL = 16
GROUP = 8
MESH = pl.DeviceIdType.MESH


def aligned(start, unit=LANES):
    return pl.multiple_of(start, unit)


def rank_kernel(owner_ref, cell_ref, request_out, slot_out):
    devices, layers = request_out.shape[0], owner_ref.shape[1]
    row = lax.broadcasted_iota(jnp.int32, (devices, layers), 0)
    owner, cell = owner_ref[...], cell_ref[...]
    found = row == owner
    matches = jnp.where(found, 1.0, 0.0).astype(jnp.bfloat16)
    first = lax.broadcasted_iota(jnp.int32, (layers, layers), 0)
    second = lax.broadcasted_iota(jnp.int32, (layers, layers), 1)
    earlier = jnp.where(first < second, 1.0, 0.0).astype(jnp.bfloat16)
    before = jnp.dot(matches, earlier, preferred_element_type=jnp.float32)
    position = jnp.sum(jnp.where(found, before, 0.0), axis=0, keepdims=True).astype(jnp.int32)
    placed = row == position
    request = jnp.zeros((devices, devices), jnp.int32)
    for shift in (0, 6, 12):
        digit = ((cell >> shift) & 63).astype(jnp.float32)
        digits = jnp.where(placed, digit, 0.0).astype(jnp.bfloat16)
        part = lax.dot_general(
            matches, digits, (((1,), (1,)), ((), ())), preferred_element_type=jnp.float32
        )
        request = request + (part.astype(jnp.int32) << shift)
    request_out[...] = request
    slot_out[...] = position * devices + owner


def rank_requests(owners, cells, devices):
    vmem = pl.BlockSpec(memory_space=pltpu.VMEM)
    return pl.pallas_call(
        rank_kernel,
        out_shape=(
            jax.ShapeDtypeStruct((devices, LANES), jnp.int32),
            jax.ShapeDtypeStruct(owners.shape, jnp.int32),
        ),
        in_specs=[vmem, vmem],
        out_specs=(vmem, vmem),
        name="rank_requests",
    )(owners, cells)


def wave_plane(comp, index, now, before, factor, out, out_shift):
    start = aligned((index + 2) * PLANE)

    def block(offset, group, tile):
        return now[comp, pl.ds(start + offset * PLANE + (group * 4 + tile) * 8, 8), :]

    sub = lax.broadcasted_iota(jnp.int32, (8, LANES), 0)
    lane = lax.broadcasted_iota(jnp.int32, (8, LANES), 1)
    zero = jnp.zeros((8, LANES), jnp.float32)
    here = [[block(0, group, tile) for tile in range(4)] for group in range(4)]

    def neighbours(values, axis, count, position):
        sums = []
        for distance in (1, 2):
            ahead = [pltpu.roll(value, distance, axis) for value in values]
            behind = [pltpu.roll(value, count - distance, axis) for value in values]
            rows = []
            for spot in range(4):
                low = ahead[spot - 1] if spot > 0 else zero
                high = behind[spot + 1] if spot < 3 else zero
                rows.append(
                    jnp.where(position < distance, low, ahead[spot])
                    + jnp.where(position >= count - distance, high, behind[spot])
                )
            sums.append(rows)
        return sums

    along_y = [neighbours([here[g][t] for g in range(4)], 0, 8, sub) for t in range(4)]
    along_z = [neighbours(here[g], 1, LANES, lane) for g in range(4)]
    for group in range(4):
        for tile in range(4):
            row = (group * 4 + tile) * 8
            near = block(-1, group, tile) + block(1, group, tile)
            far = block(-2, group, tile) + block(2, group, tile)
            near = near + (along_y[tile][0][group] + along_z[group][0][tile])
            far = far + (along_y[tile][1][group] + along_z[group][1][tile])
            centre = here[group][tile]
            laplace = NEAR * near + FAR * far - 7.5 * centre
            place = pl.ds(aligned(index * PLANE) + row, 8)
            result = 2.0 * centre - before[comp, pl.ds(aligned(before_start(before, index)) + row, 8), :]
            out[comp, pl.ds(aligned((index + out_shift) * PLANE) + row, 8), :] = (
                result + factor[place, :] * laplace
            )


def before_start(before, index):
    shift = 2 if before.shape[1] == 20 * PLANE else 0
    return (index + shift) * PLANE


def y_edges(comp, index, source, low_out, high_out):
    start = aligned((index + 2) * PLANE)
    for tile in range(4):
        first = source[comp, pl.ds(start + tile * 8, 8), :]
        last = source[comp, pl.ds(start + 96 + tile * 8, 8), :]
        low_out[comp, index, 2 * tile : 2 * tile + 2, :] = first[0:2]
        high_out[comp, index, 2 * tile : 2 * tile + 2, :] = last[6:8]


def y_corrections(comp, index, low, high, low_weight, high_weight, factor, out, out_shift):
    sub = lax.broadcasted_iota(jnp.int32, (8, LANES), 0)
    start = aligned((index + out_shift) * PLANE)
    here = aligned(index * PLANE)
    lows = low[comp, index] * low_weight
    highs = high[comp, index] * high_weight
    for tile in range(4):
        far_row, near_row = lows[2 * tile : 2 * tile + 1], lows[2 * tile + 1 : 2 * tile + 2]
        term = jnp.where(
            sub == 0, NEAR * near_row + FAR * far_row, jnp.where(sub == 1, FAR * near_row, 0.0)
        )
        place = pl.ds(start + tile * 8, 8)
        out[comp, place, :] = out[comp, place, :] + factor[pl.ds(here + tile * 8, 8), :] * term
        near_row, far_row = highs[2 * tile : 2 * tile + 1], highs[2 * tile + 1 : 2 * tile + 2]
        term = jnp.where(
            sub == 7, NEAR * near_row + FAR * far_row, jnp.where(sub == 6, FAR * near_row, 0.0)
        )
        place = pl.ds(start + 96 + tile * 8, 8)
        out[comp, place, :] = out[comp, place, :] + factor[pl.ds(here + 96 + tile * 8, 8), :] * term


def grid_kernel(
    now_hbm, before_hbm, factor_hbm, request, disp_raw, ids_raw, shear_raw, lame_raw, scale_raw, live,
    after_hbm, disp_all, ids_all, params_all, reply_out,
    now, mid, after, before, factor, y_sent, y_got, asked_x, asked_t, asked_y, rows_vmem,
    rows_smem, found, found_x, found_t, disp_own, ids_own, params_own, send_sems, recv_sems, local_sems,
    store_sems,
):
    gx, gy = lax.axis_index("gx"), lax.axis_index("gy")
    count_x, count_y = lax.axis_size("gx"), lax.axis_size("gy")
    planes = factor.shape[0] // PLANE
    edge = 2 * PLANE
    inside = pl.ds(edge, planes * PLANE)

    loads = [
        pltpu.make_async_copy(now_hbm, now.at[:, inside, :], local_sems.at[0]),
        pltpu.make_async_copy(before_hbm, before, local_sems.at[1]),
        pltpu.make_async_copy(factor_hbm, factor, local_sems.at[2]),
    ]
    for load in loads:
        load.start()

    barrier = pltpu.get_barrier_semaphore()
    for step in range(1, count_x):
        peer = lax.rem(gx + step, count_x)
        pl.semaphore_signal(barrier, inc=1, device_id=(peer, gy), device_id_type=MESH)
    for step in range(1, count_y):
        peer = lax.rem(gy + step, count_y)
        pl.semaphore_signal(barrier, inc=1, device_id=(gx, peer), device_id_type=MESH)
    pl.semaphore_wait(barrier, count_x + count_y - 2)

    used = [0]

    def send(source, target, device):
        slot = used[0]
        used[0] += 1
        copy = pltpu.make_async_remote_copy(
            src_ref=source,
            dst_ref=target,
            send_sem=send_sems.at[slot],
            recv_sem=recv_sems.at[slot],
            device_id=device,
            device_id_type=MESH,
        )
        copy.start()
        return copy

    right, left = lax.rem(gx + 1, count_x), lax.rem(gx + count_x - 1, count_x)
    upper, lower = lax.rem(gy + 1, count_y), lax.rem(gy + count_y - 1, count_y)
    top = (planes - 2) * PLANE

    def x_halo(source, shift, target, comp):
        return [
            send(
                source.at[comp, pl.ds(top + shift, edge), :],
                target.at[comp, pl.ds(0, edge), :],
                (right, gy),
            ),
            send(
                source.at[comp, pl.ds(shift, edge), :],
                target.at[comp, pl.ds(edge + planes * PLANE, edge), :],
                (left, gy),
            ),
        ]

    def y_halo(step, comp):
        return [
            send(y_sent.at[step, 1, comp], y_got.at[step, 0, comp], (gx, upper)),
            send(y_sent.at[step, 0, comp], y_got.at[step, 1, comp], (gx, lower)),
        ]

    def each_plane(comp, ranges, body):
        for low, high in ranges:
            lax.fori_loop(low, high, lambda index, c: (body(comp, index), c)[1], 0)

    def edges(step, source, comp):
        each_plane(
            comp,
            [(0, planes)],
            lambda comp, index: y_edges(comp, index, source, y_sent.at[step, 0], y_sent.at[step, 1]),
        )

    def clear_outside(target, comp):
        @pl.when(gx == 0)
        def _():
            target[comp, 0:edge, :] = jnp.zeros((edge, LANES), jnp.float32)

        @pl.when(gx == count_x - 1)
        def _():
            target[comp, edge + planes * PLANE :, :] = jnp.zeros((edge, LANES), jnp.float32)

    low_weight = jnp.where(gy == 0, 0.0, 1.0).astype(jnp.float32)
    high_weight = jnp.where(gy == count_y - 1, 0.0, 1.0).astype(jnp.float32)

    first_x = [x_halo(now_hbm, 0, now, comp) for comp in range(3)]
    asks = []
    for step in range(1, count_x):
        peer = lax.rem(gx + step, count_x)
        asks.append(send(request.at[peer], asked_x.at[gx], (peer, gy)))
    asked_x[gx] = request[gx]
    loads[0].wait()
    first_y = []
    for comp in range(3):
        edges(0, now, comp)
        first_y.append(y_halo(0, comp))
    for comp in range(3):
        for tile in range(disp_raw.shape[1]):
            disp_own[comp : comp + 1, tile * LANES : (tile + 1) * LANES] = disp_raw[comp, tile]
    stripes = ids_raw.shape[1] // count_y
    for turn in range(count_y):
        every = pl.ds(turn, stripes, stride=count_y)
        for corner in range(8):
            here = slice(corner * stripes, (corner + 1) * stripes)
            ids_own[turn, here, :] = ids_raw[corner, every, :]
        ids_own[turn, 8 * stripes :, :] = jnp.full((8, LANES), live[0, 0], jnp.int32)
        for index, raw in enumerate((shear_raw, lame_raw, scale_raw)):
            here = slice(index * stripes, (index + 1) * stripes)
            params_own[turn, here, :] = raw[every, :]
    bulk = []
    for step in range(1, count_y):
        peer = lax.rem(gy + step, count_y)
        bulk.append(send(disp_own, disp_all.at[gy], (gx, peer)))
        bulk.append(send(ids_own.at[step], ids_all.at[gy], (gx, peer)))
        bulk.append(send(params_own.at[step], params_all.at[gy], (gx, peer)))
    own = [
        pltpu.make_async_copy(disp_own, disp_all.at[gy], local_sems.at[3]),
        pltpu.make_async_copy(ids_own.at[0], ids_all.at[gy], local_sems.at[4]),
        pltpu.make_async_copy(params_own.at[0], params_all.at[gy], local_sems.at[5]),
    ]
    for copy in own:
        copy.start()
    loads[1].wait()
    loads[2].wait()

    def step_of(source, previous, target, shift):
        return lambda comp, index: wave_plane(comp, index, source, previous, factor, target, shift)

    def fix(step, target, shift, comp):
        each_plane(
            comp,
            [(0, planes)],
            lambda comp, index: y_corrections(
                comp, index, y_got.at[step, 0], y_got.at[step, 1], low_weight, high_weight,
                factor, target, shift,
            ),
        )

    inner, outer = [(2, planes - 2)], [(0, 2), (planes - 2, planes)]
    first = step_of(now, before, mid, 2)
    second = step_of(mid, now, after, 0)
    for comp in range(3):
        each_plane(comp, inner, first)
    second_x, second_y, passes = [], [], []
    for comp in range(3):
        for copy in first_x[comp]:
            copy.wait()
        clear_outside(now, comp)
        each_plane(comp, outer, first)
        for copy in first_y[comp]:
            copy.wait()
        fix(0, mid, 2, comp)
        second_x.append(x_halo(mid, edge, mid, comp))
        edges(1, mid, comp)
        second_y.append(y_halo(1, comp))
        if comp == 0:
            for copy in asks:
                copy.wait()
            for peer in range(count_y):
                asked_t[peer] = asked_x[:, peer, :]
            for step in range(1, count_y):
                peer = lax.rem(gy + step, count_y)
                passes.append(send(asked_t.at[peer], asked_y.at[gy], (gx, peer)))
            asked_y[gy] = asked_t[gy]
        each_plane(comp, inner, second)
    for copy in passes:
        copy.wait()
    cell = asked_y[...]
    plane, row, col = cell >> 14, (cell >> 9) & 31, cell & 511
    rows_vmem[...] = (((plane * 4 + (row >> 3)) * 4 + (col >> 7)) * 8 + (row & 7)) * LANES + (
        col & (LANES - 1)
    )
    to_smem = pltpu.make_async_copy(rows_vmem, rows_smem, local_sems.at[6])
    to_smem.start()
    stores = []
    for comp in range(3):
        for copy in second_x[comp]:
            copy.wait()
        clear_outside(mid, comp)
        each_plane(comp, outer, second)
        for copy in second_y[comp]:
            copy.wait()
        fix(1, after, 0, comp)
        store = pltpu.make_async_copy(after.at[comp], after_hbm.at[comp], store_sems.at[comp])
        store.start()
        stores.append(store)
    to_smem.wait()

    lane = lax.broadcasted_iota(jnp.int32, (1, LANES), 1)
    capacity = LANES // SLOTS

    unroll = 8

    def find(part):
        def run(chunk, carry):
            for step in range(unroll):
                source = chunk * unroll + step
                held = jnp.zeros((1, LANES), jnp.float32)
                for position in range(capacity):
                    place = rows_smem[part, source, position]
                    line = place >> 7
                    for comp in range(3):
                        spot = position * SLOTS + comp
                        values = after[comp, pl.ds(line, 1), :]
                        shift = (spot - place) & (LANES - 1)
                        held = jnp.where(lane == spot, pltpu.roll(values, shift, 1), held)
                found[part, pl.ds(source, 1), :] = held
            return carry

        lax.fori_loop(0, count_x // unroll, run, 0)

    answers = []
    for step in range(1, count_y):
        peer = lax.rem(gy + step, count_y)
        find(peer)
        answers.append(send(found.at[peer], found_x.at[gy], (gx, peer)))
    find(gy)
    found_x[gy] = found[gy]
    for copy in answers:
        copy.wait()
    for peer in range(count_x):
        found_t[peer] = found_x[:, peer, :]
    finals = []
    for step in range(1, count_x):
        peer = lax.rem(gx + step, count_x)
        finals.append(send(found_t.at[peer], reply_out.at[gx], (peer, gy)))
    reply_out[gx] = found_t[gx]
    for copy in finals + bulk + own:
        copy.wait()
    for store in stores:
        store.wait()


def grid_steps(now, before, factor, request, disp, ids, params, live, count_x, count_y):
    rows = factor.shape[0]
    f32, i32 = jnp.float32, jnp.int32
    hbm = pl.BlockSpec(memory_space=pl.ANY)
    vmem = pl.BlockSpec(memory_space=pltpu.VMEM)
    halo_rows = rows + 4 * PLANE
    copies = 24 + 3 * (count_y - 1) + 2 * (count_x - 1) + 2 * (count_y - 1)
    planes = rows // PLANE
    stripes = ids.shape[1] // count_y
    return pl.pallas_call(
        grid_kernel,
        out_shape=(
            jax.ShapeDtypeStruct(now.shape, f32),
            jax.ShapeDtypeStruct((count_y, 3, disp.shape[1] * LANES), f32),
            jax.ShapeDtypeStruct((count_y, ID_ROWS, LANES), i32),
            jax.ShapeDtypeStruct((count_y, 3 * stripes, LANES), f32),
            jax.ShapeDtypeStruct(request.shape, f32),
        ),
        in_specs=[hbm, hbm, hbm] + [vmem] * 6 + [pl.BlockSpec(memory_space=pltpu.SMEM)],
        out_specs=(hbm, hbm, hbm, hbm, vmem),
        scratch_shapes=[
            pltpu.VMEM((3, halo_rows, LANES), f32),
            pltpu.VMEM((3, halo_rows, LANES), f32),
            pltpu.VMEM((3, rows, LANES), f32),
            pltpu.VMEM((3, rows, LANES), f32),
            pltpu.VMEM((rows, LANES), f32),
            pltpu.VMEM((2, 2, 3, planes, 8, LANES), f32),
            pltpu.VMEM((2, 2, 3, planes, 8, LANES), f32),
            pltpu.VMEM((count_x, count_y, LANES), i32),
            pltpu.VMEM((count_y, count_x, LANES), i32),
            pltpu.VMEM((count_y, count_x, LANES), i32),
            pltpu.VMEM((count_y, count_x, LANES), i32),
            pltpu.SMEM((count_y, count_x, LANES), i32),
            pltpu.VMEM((count_y, count_x, LANES), f32),
            pltpu.VMEM((count_y, count_x, LANES), f32),
            pltpu.VMEM((count_x, count_y, LANES), f32),
            pltpu.VMEM((3, disp.shape[1] * LANES), f32),
            pltpu.VMEM((count_y, ID_ROWS, LANES), i32),
            pltpu.VMEM((count_y, 3 * stripes, LANES), f32),
            pltpu.SemaphoreType.DMA((copies,)),
            pltpu.SemaphoreType.DMA((copies,)),
            pltpu.SemaphoreType.DMA((8,)),
            pltpu.SemaphoreType.DMA((3,)),
        ],
        compiler_params=pltpu.CompilerParams(
            vmem_limit_bytes=VMEM_LIMIT, collective_id=1, has_side_effects=True
        ),
        name="grid_steps",
    )(now, before, factor, request, disp, ids, *params, live)


def gradient_signs(corner):
    lane = lax.broadcasted_iota(jnp.int32, (1, LANES), 1)
    signs = jnp.zeros((1, LANES), jnp.float32)
    for direction in range(3):
        value = 0.25 if (corner >> direction) & 1 else -0.25
        inside = (lane >= 3 * direction) & (lane < 3 * direction + 3)
        signs = jnp.where(inside, value, signs)
    return signs


def rows_of(values):
    count = values.shape[0]
    padded = jnp.concatenate(
        [values, jnp.zeros((SLOTS - count, LANES), jnp.float32)], axis=0
    )
    return padded.T


def box_kernel(
    layer_ref, slot_ref, ids_hbm, disp_ref, params_ref, reply_ref, field_in,
    out_ref, field_out, table, rows, layer_rows, reply_rows, field, counts, *rest,
):
    ids, sems, count_sem, field_sem = rest[:8], rest[8], rest[9], rest[10]
    owners, _, own = disp_ref.shape
    stripe = ids[0].shape[0] // owners
    span = ID_ROWS * LANES
    copies = []
    for part in range(owners):
        copies.append(
            pltpu.make_async_copy(
                ids_hbm.at[pl.ds(part * span + 8 * stripe, 1024)],
                counts.at[pl.ds(part * 1024, 1024)],
                count_sem.at[part],
            )
        )
        for corner in range(8):
            copies.append(
                pltpu.make_async_copy(
                    ids_hbm.at[pl.ds(part * span + corner * stripe, stripe)],
                    ids[corner].at[pl.ds(part * stripe, stripe)],
                    sems.at[part, corner],
                )
            )
    for copy in copies:
        copy.start()
    field_load = pltpu.make_async_copy(field_in, field, field_sem.at[0])
    field_load.start()

    def build(part, carry):
        for tile in range(own // LANES):
            block = disp_ref[part, :, tile * LANES : (tile + 1) * LANES]
            lines = rows_of(jnp.concatenate([block, block, block], axis=0))
            table[pl.ds(aligned(part * own + tile * LANES), LANES), 0:SLOTS] = lines
        return carry

    lax.fori_loop(0, owners, build, 0)
    field_load.wait()
    field_store = pltpu.make_async_copy(field, field_out, field_sem.at[1])
    field_store.start()
    signs = [gradient_signs(corner) for corner in range(8)]
    mine = lax.axis_index("gy")

    def live_of(part):
        count = counts[part * 1024]
        whole = count // LANES
        turn = lax.rem(mine - part + owners, owners)
        tiles = (whole + owners - 1 - turn) // owners
        partial = jnp.where(whole % owners == turn, count % LANES, 0)
        return tiles * LANES + partial


    for part in range(owners):
        for copy in copies[9 * part : 9 * part + 9]:
            copy.wait()

        def gather(chunk, carry, part=part):
            base = part * stripe + chunk * GATHER_UNROLL
            for step in range(GATHER_UNROLL):
                slot = base + step
                ends = [table[pl.ds(ids[corner][slot], 1), :] for corner in range(8)]
                spans = [ends[corner] - ends[7 - corner] for corner in range(4)]
                rows[pl.ds(slot, 1), :] = (spans[0] * signs[0] + spans[1] * signs[1]) + (
                    spans[2] * signs[2] + spans[3] * signs[3]
                )
            return carry

        lax.fori_loop(0, (live_of(part) + GATHER_UNROLL - 1) // GATHER_UNROLL, gather, 0)

    def layer_ends(chunk, carry):
        base = chunk * LAYER_UNROLL
        for step in range(LAYER_UNROLL):
            node = layer_ref[0, base + step]
            layer_rows[pl.ds(base + step, 1), :] = table[pl.ds(node, 1), :]
        return carry

    layers = layer_rows.shape[0]
    lax.fori_loop(0, layers // LAYER_UNROLL, layer_ends, 0)

    def clear(chunk, carry):
        zero = jnp.zeros((LANES, LANES), jnp.float32)
        table[pl.ds(aligned(chunk * LANES), LANES), :] = zero
        return carry

    lax.fori_loop(0, table.shape[0] // LANES, clear, 0)
    lane = lax.broadcasted_iota(jnp.int32, (1, LANES), 1)
    total = table
    tiles = stripe // LANES

    def scatter_part(part, outer_carry):
        live = live_of(part)

        def element(tile, carry):
            start = aligned(part * stripe + tile * LANES)
            grads = rows[pl.ds(start, LANES), 0:SLOTS].T
            slope = [[grads[3 * j + i : 3 * j + i + 1] for j in range(3)] for i in range(3)]
            s00, s11, s22 = slope[0][0], slope[1][1], slope[2][2]
            s01 = 0.5 * (slope[0][1] + slope[1][0])
            s02 = 0.5 * (slope[0][2] + slope[2][0])
            s12 = 0.5 * (slope[1][2] + slope[2][1])
            trace = s00 + s11 + s22
            mean = trace / 3.0
            d00, d11, d22 = s00 - mean, s11 - mean, s22 - mean
            invariant = d00 * d00 + d11 * d11 + d22 * d22
            invariant = invariant + 2.0 * (s01 * s01 + s02 * s02 + s12 * s12)
            shear = params_ref[part, pl.ds(tile, 1), :]
            lame = params_ref[part, pl.ds(tiles + tile, 1), :]
            scale = params_ref[part, pl.ds(2 * tiles + tile, 1), :]
            softened = 2.0 * shear / (1.0 + invariant / scale)
            volume = lame * trace
            index = tile * LANES + lane

            def signed(value):
                return jnp.where(index < live, -0.25 * value, 0.0)

            p00 = signed(volume + softened * s00)
            p11 = signed(volume + softened * s11)
            p22 = signed(volume + softened * s22)
            p01, p02, p12 = signed(softened * s01), signed(softened * s02), signed(softened * s12)
            pad = jnp.zeros((GROUP - 3, LANES), jnp.float32)
            sides = [
                jnp.concatenate(column + [pad], axis=0)
                for column in ([p00, p01, p02], [p01, p11, p12], [p02, p12, p22])
            ]
            ends = []
            for corner in range(4):
                term = sides[0] if corner & 1 else -sides[0]
                term = term + sides[1] if corner & 2 else term - sides[1]
                ends.append(term - sides[2])
            ends += [-ends[7 - corner] for corner in range(4, 8)]
            rows[pl.ds(start, LANES), 0 : 8 * GROUP] = jnp.concatenate(ends, axis=0).T
            return carry

        lax.fori_loop(0, (live + LANES - 1) // LANES, element, 0)

        def scatter(chunk, carry):
            base = part * stripe + chunk * SCATTER_UNROLL
            for step in range(SCATTER_UNROLL):
                line = rows[pl.ds(base + step, 1), :]
                for corner in range(8):
                    own_lanes = slice(corner * GROUP, (corner + 1) * GROUP)
                    total[pl.ds(ids[corner][base + step], 1), own_lanes] = line[:, own_lanes]
            return carry

        lax.fori_loop(0, (live + SCATTER_UNROLL - 1) // SCATTER_UNROLL, scatter, 0)
        return outer_carry

    lax.fori_loop(0, owners, scatter_part, 0)
    devices = reply_ref.shape[0]
    for position in range(LANES // SLOTS):
        values = reply_ref[...]
        if position:
            values = pltpu.roll(values, LANES - position * SLOTS, 1)
        reply_rows[position * devices : (position + 1) * devices, :] = values
    inside = lane < 3

    def layer(chunk, carry):
        base = chunk * LAYER_UNROLL
        steps = range(LAYER_UNROLL)
        nodes = [layer_ref[0, base + step] for step in steps]
        held = [total[pl.ds(node, 1), :] for node in nodes]
        for step in steps:
            reply = reply_rows[pl.ds(slot_ref[0, base + step], 1), :]
            gap = reply - layer_rows[pl.ds(base + step, 1), :]
            held[step] = held[step] + jnp.where(inside, PENALTY * gap, 0.0)
        for step in steps:
            total[pl.ds(nodes[step], 1), :] = held[step]
        return carry

    lax.fori_loop(0, layers // LAYER_UNROLL, layer, 0)

    def fold(part, carry):
        for tile in range(own // LANES):
            start = aligned(part * own + tile * LANES)
            block = total[pl.ds(start, LANES), 0 : 8 * GROUP].T
            terms = [block[corner * GROUP : corner * GROUP + GROUP] for corner in range(8)]
            while len(terms) > 1:
                terms = [a + b for a, b in zip(terms[0::2], terms[1::2])]
            for comp in range(3):
                line = comp * (own // LANES) + tile
                out_ref[part, line : line + 1, :] = terms[0][comp : comp + 1]
        return carry

    lax.fori_loop(0, owners, fold, 0)
    field_store.wait()


def box_forces(layer_ids, slot_index, ids, disp, params, replies, field):
    owners, _, own = disp.shape
    slots = params.shape[1] * LANES // 3 * owners
    layers = layer_ids.shape[1]
    smem = pl.BlockSpec(memory_space=pltpu.SMEM)
    vmem = pl.BlockSpec(memory_space=pltpu.VMEM)
    hbm = pl.BlockSpec(memory_space=pl.ANY)
    f32, i32 = jnp.float32, jnp.int32
    return pl.pallas_call(
        box_kernel,
        out_shape=(
            jax.ShapeDtypeStruct((owners, 3 * own // LANES, LANES), f32),
            jax.ShapeDtypeStruct(field.shape, f32),
        ),
        in_specs=[smem, smem, hbm, vmem, vmem, vmem, hbm],
        out_specs=(vmem, hbm),
        scratch_shapes=[
            pltpu.VMEM((owners * own, LANES), f32),
            pltpu.VMEM((slots, LANES), f32),
            pltpu.VMEM((layers, LANES), f32),
            pltpu.VMEM((replies.shape[0] * (LANES // SLOTS), LANES), f32),
            pltpu.VMEM(field.shape, f32),
            pltpu.SMEM((owners * 1024,), i32),
        ]
        + [pltpu.SMEM((slots,), i32)] * 8
        + [
            pltpu.SemaphoreType.DMA((owners, 8)),
            pltpu.SemaphoreType.DMA((owners,)),
            pltpu.SemaphoreType.DMA((2,)),
        ],
        compiler_params=pltpu.CompilerParams(vmem_limit_bytes=VMEM_LIMIT),
        name="box_forces",
    )(layer_ids, slot_index, ids, disp, params, replies, field)


def sum_kernel(
    parts_hbm, out_ref, mine, near, sums, far, send_sems, recv_sems, local_sem
):
    gx, gy = lax.axis_index("gx"), lax.axis_index("gy")
    pairs = lax.axis_size("gy") // 2
    side, place = lax.rem(gy, 2), gy // 2
    other = 2 * place + 1 - side
    load = pltpu.make_async_copy(parts_hbm.at[:, side], mine, local_sem.at[0])
    load.start()
    barrier = pltpu.get_barrier_semaphore()
    pl.semaphore_signal(barrier, inc=1, device_id=(gx, other), device_id_type=MESH)
    for step in range(1, pairs):
        peer = 2 * lax.rem(place + step, pairs) + side
        pl.semaphore_signal(barrier, inc=1, device_id=(gx, peer), device_id_type=MESH)
    pl.semaphore_wait(barrier, pairs)
    swap = pltpu.make_async_remote_copy(
        src_ref=parts_hbm.at[:, 1 - side],
        dst_ref=near,
        send_sem=send_sems.at[0],
        recv_sem=recv_sems.at[0],
        device_id=(gx, other),
        device_id_type=MESH,
    )
    swap.start()
    load.wait()
    swap.wait()
    copies = []
    for step in range(1, pairs):
        target = lax.rem(place + step, pairs)
        sums[step] = mine[target] + near[target]
        copy = pltpu.make_async_remote_copy(
            src_ref=sums.at[step],
            dst_ref=far.at[step],
            send_sem=send_sems.at[step],
            recv_sem=recv_sems.at[step],
            device_id=(gx, 2 * target + side),
            device_id_type=MESH,
        )
        copy.start()
        copies.append(copy)
    total = mine[place] + near[place]
    for step, copy in enumerate(copies, 1):
        copy.wait()
        total = total + far[step]
    out_ref[...] = total


def sum_forces(parts):
    count, rows, _ = parts.shape
    block = pltpu.VMEM((count // 2, rows, LANES), jnp.float32)
    return pl.pallas_call(
        sum_kernel,
        out_shape=jax.ShapeDtypeStruct((rows, LANES), jnp.float32),
        in_specs=[pl.BlockSpec(memory_space=pl.ANY)],
        out_specs=pl.BlockSpec(memory_space=pltpu.VMEM),
        scratch_shapes=[
            block,
            block,
            block,
            block,
            pltpu.SemaphoreType.DMA((count // 2,)),
            pltpu.SemaphoreType.DMA((count // 2,)),
            pltpu.SemaphoreType.DMA((1,)),
        ],
        compiler_params=pltpu.CompilerParams(
            vmem_limit_bytes=VMEM_LIMIT, collective_id=2, has_side_effects=True
        ),
        name="sum_forces",
    )(parts.reshape(count // 2, 2, rows, LANES))


def tiled_rows(field):
    lead, (rows, cols) = field.shape[:-2], field.shape[-2:]
    tiles = field.reshape(lead + (rows // 8, 8, cols // LANES, LANES))
    tiles = jnp.swapaxes(tiles, -3, -2)
    return tiles.reshape(lead[:-1] + (-1, LANES))


def untiled_rows(values, shape):
    rows, cols = shape[-2:]
    tiles = values.reshape(shape[:-2] + (rows // 8, cols // LANES, 8, LANES))
    return jnp.swapaxes(tiles, -3, -2).reshape(shape)


def on_device(
    grid_now,
    grid_before,
    wave_factor,
    layer_owner,
    layer_cell,
    box_now,
    box_before,
    node_mass,
    corner_nodes,
    live_counts,
    shear_modulus,
    lame_lambda,
    strain_scale,
    layer_nodes,
):
    count_x, count_y = lax.axis_size("gx"), lax.axis_size("gy")
    devices = count_x * count_y
    own_disp = box_now.reshape(3, -1)

    request, slot_index = rank_requests(
        layer_owner.reshape(1, -1), layer_cell.reshape(1, -1), devices
    )
    lines = (-1, LANES)

    after, all_disp, all_ids, all_params, replies = grid_steps(
        tiled_rows(grid_now),
        tiled_rows(grid_before),
        tiled_rows(wave_factor),
        request.reshape(count_x, count_y, LANES),
        box_now.reshape(3, -1, 1, LANES),
        corner_nodes.reshape(8, -1, LANES),
        [values.reshape(lines) for values in (shear_modulus, lame_lambda, strain_scale)],
        live_counts,
        count_x,
        count_y,
    )
    node_term, after = box_forces(
        layer_nodes,
        slot_index,
        all_ids.reshape(-1),
        all_disp,
        all_params,
        replies.reshape(devices, LANES),
        after,
    )
    summed = sum_forces(node_term).reshape(own_disp.shape)
    box_after = 2.0 * own_disp - box_before.reshape(3, -1) + STEP_SQUARE / node_mass * summed
    return (untiled_rows(after, grid_now.shape), box_after.reshape(box_now.shape))


def solution(mesh):
    return jax.shard_map(
        on_device,
        mesh=mesh,
        in_specs=(
            P(None, "gx", "gy", None),
            P(None, "gx", "gy", None),
            P("gx", "gy", None),
            P("gx", "gy", None),
            P("gx", "gy"),
            P(None, "gx", "gy"),
            P(None, "gx", "gy"),
            P("gx", "gy"),
            P(None, "gx", "gy"),
            P("gx", "gy"),
            P("gx", "gy"),
            P("gx", "gy"),
            P("gx", "gy"),
            P("gx", "gy"),
        ),
        out_specs=(P(None, "gx", "gy", None), P(None, "gx", "gy")),
        check_vma=False,
    )
```
